256 devices in a mesh: seq: 32 (over z, y), head: 8 (over x, core).
Axes of the slice: x: 4, y: 4, z: 8, core: 2. Of those that a mesh axis runs over, the one named last changes fastest.
Arguments:
- q_data: bfloat16 [32768, 6144], P(('seq', 'head')), may hold values from -20 to 20
- k_data: bfloat16 [32768, 6144], P(('seq', 'head')), may hold values from -20 to 20
- v_data: bfloat16 [32768, 6144], P(('seq', 'head')), may hold values from -6 to 6
- q_exp: int32 [256, 48], P(('seq', 'head')), may hold values from -1 to 1
- k_exp: int32 [256, 48], P(('seq', 'head')), may hold values from -1 to 1
- v_exp: int32 [256, 48], P(('seq', 'head')), may hold values from -1 to 1
- extents: int32 [48, 3], replicated, may hold values from 0 to 3, as said below
Outputs:
- attended: bfloat16 [32768, 6144], P(('seq', 'head'))
The draws below stay inside these ranges and needn't reach their ends.
Inputs may be any that keep to these rules, and one draw needn't show every extreme that they name: `extents`: column 0 is 0 or 1, column 1 at most 3, column 2 at most 1; some head has all three largest values.
All inputs are finite; a program needn't handle non-finite values.
Results may differ from the reference program's by a relative error of at most 0.0049.
Values may be sent and summed in bfloat16 or wider, within the bound.
A program may use at most 128 MiB of HBM per device.

```python
import math
import jax
import jax.numpy as jnp
from jax import lax

H = 48
HD = 128
TILE = 128
HT = 4
WT = 2
TOKENS = 32768
TILES = 256
N_SEQ = 32


def draw_q_data(key, part):
    key = jax.random.fold_in(key, 1)
    shape = (TOKENS, H * HD)
    values = jnp.clip(jax.random.normal(key, shape), -6.0, 6.0)
    return values.astype(jnp.bfloat16)


def draw_k_data(key, part):
    key = jax.random.fold_in(key, 2)
    shape = (TOKENS, H * HD)
    own = jnp.clip(jax.random.normal(key, shape), -6.0, 6.0)
    values = own
    return values.astype(jnp.bfloat16)


def draw_extents(key, part):
    key = jax.random.fold_in(key, 3)
    frames_ext = jax.random.randint(jax.random.fold_in(key, 1), (H,), 0, 2)
    height_ext = jax.random.randint(jax.random.fold_in(key, 2), (H,), 0, HT)
    width_ext = jax.random.randint(jax.random.fold_in(key, 3), (H,), 0, WT)
    picked = jax.random.randint(jax.random.fold_in(key, 4), (), 0, H)
    is_picked = jnp.arange(H, dtype=jnp.int32) == picked
    frames_ext = jnp.where(is_picked, 1, frames_ext)
    height_ext = jnp.where(is_picked, HT - 1, height_ext)
    width_ext = jnp.where(is_picked, WT - 1, width_ext)
    return jnp.stack([frames_ext, height_ext, width_ext], axis=1).astype(jnp.int32)


def place_ends(entries, rng, smallest, largest):
    shape = entries.shape
    index_at = [jax.random.randint(jax.random.fold_in(rng, axis), (), 0, shape[axis]) for axis in range(len(shape))]
    entries = entries.at[tuple(index_at)].set(smallest)
    longest = shape.index(max(shape))
    index_at[longest] = (index_at[longest] + 1) % shape[longest]
    return entries.at[tuple(index_at)].set(largest)


def level_of(rng, shape, cuts, low, largest):
    def one(position, shards_of):
        draws = jax.random.uniform(jax.random.fold_in(jax.random.fold_in(rng, 6), position), (shards_of,), jnp.float32, low / len(cuts), largest / len(cuts))
        return jnp.repeat(jnp.exp(draws), shape[position] // shards_of).reshape((-1,) + (1,) * (len(shape) - position - 1))

    loudness = one(*cuts[0])
    for cut in cuts[1:]:
        loudness = loudness * one(*cut)
    return loudness


def centred(stream_key, shape, scale, limit, cuts=(), held_as=jnp.bfloat16):
    loudness = level_of(stream_key, shape, cuts, -0.22, 0.18) if cuts else 1.0
    array = jax.random.normal(stream_key, shape, jnp.float32) * scale * loudness
    return jnp.minimum(jnp.maximum(array, -limit), limit).astype(held_as)


def setup_inputs(seed: int = 0) -> dict:
    seeds = jax.random.split(jax.random.key(seed), 8)
    return {
        "q_data": draw_q_data(jax.random.fold_in(seeds[7], 71), 0),
        "k_data": draw_k_data(jax.random.fold_in(seeds[7], 71), 0),
        "v_data": centred(seeds[2], (TOKENS, H * HD), 1.0, 6.0, ((0, 256),)),
        "q_exp": place_ends(jax.random.randint(seeds[3], (TILES, H), -1, 2), jax.random.fold_in(seeds[3], 1), -1, 1).astype(jnp.int32),
        "k_exp": place_ends(jax.random.randint(seeds[4], (TILES, H), -1, 2), jax.random.fold_in(seeds[4], 1), -1, 1).astype(jnp.int32),
        "v_exp": place_ends(jax.random.randint(seeds[5], (TILES, H), -1, 2), jax.random.fold_in(seeds[5], 1), -1, 1).astype(jnp.int32),
        "extents": draw_extents(jax.random.fold_in(seeds[7], 71), 0),
    }


def allowed_pairs(extent, frame_index, frame_total, frame_tokens):
    row_index = jnp.arange(frame_tokens, dtype=jnp.int32)
    key_index = jnp.arange(3 * frame_tokens, dtype=jnp.int32)
    query_tile = row_index // TILE
    key_tile = key_index % frame_tokens // TILE
    frame_step = key_index // frame_tokens - 1
    near_frame = (jnp.abs(frame_step) <= extent[0]) & (frame_index + frame_step >= 0) & (frame_index + frame_step < frame_total)
    near_height = jnp.abs(query_tile[:, None] // WT - key_tile[None, :] // WT) <= extent[1]
    near_width = jnp.abs(query_tile[:, None] % WT - key_tile[None, :] % WT) <= extent[2]
    return near_frame[None, :] & near_height & near_width

def attend_head(queries, keys_near, values_near, extent, frame_index, frame_total):
    frame_tokens = queries.shape[0]
    scores = lax.dot_general(queries, keys_near, (((1,), (1,)), ((), ())), preferred_element_type=jnp.float32)
    scores = scores * (1.0 / math.sqrt(queries.shape[1]))
    scores = jnp.where(allowed_pairs(extent, frame_index, frame_total, frame_tokens), scores, -1e+30)
    peak = lax.optimization_barrier(jnp.max(scores, axis=1, keepdims=True))
    weights = jnp.exp(scores - peak)
    weights = weights / lax.optimization_barrier(jnp.sum(weights, axis=1, keepdims=True))
    return jnp.dot(weights.astype(jnp.bfloat16), values_near, preferred_element_type=jnp.float32).astype(jnp.bfloat16)

def dequantize(data, exponents):
    tiles = exponents.shape[0]
    scale = jnp.exp2(exponents.astype(jnp.float32))
    blocks = data.reshape(tiles, TILE, H, HD).astype(jnp.float32) * scale[:, None, :, None]
    return blocks.astype(jnp.bfloat16)

def reference(q_data, k_data, v_data, q_exp, k_exp, v_exp, extents):
    frame_tokens = HT * WT * TILE
    queries = dequantize(q_data, q_exp).reshape(N_SEQ, frame_tokens, H, HD)
    keys_all = dequantize(k_data, k_exp).reshape(N_SEQ, frame_tokens, H, HD)
    values_all = dequantize(v_data, v_exp).reshape(N_SEQ, frame_tokens, H, HD)
    blank = jnp.zeros((1, frame_tokens, H, HD), jnp.bfloat16)
    keys_pad = jnp.concatenate([blank, keys_all, blank], axis=0)
    values_pad = jnp.concatenate([blank, values_all, blank], axis=0)

    def one_frame(frame_index):
        query_frame = lax.dynamic_index_in_dim(queries, frame_index, 0, keepdims=False)
        key_frames = lax.dynamic_slice_in_dim(keys_pad, frame_index, 3, 0).reshape(3 * frame_tokens, H, HD)
        value_frames = lax.dynamic_slice_in_dim(values_pad, frame_index, 3, 0).reshape(3 * frame_tokens, H, HD)

        def one_head(pieces):
            return attend_head(pieces[0], pieces[1], pieces[2], pieces[3], frame_index, N_SEQ)
        result = lax.map(one_head, (jnp.moveaxis(query_frame, 1, 0), jnp.moveaxis(key_frames, 1, 0), jnp.moveaxis(value_frames, 1, 0), extents))
        return jnp.moveaxis(result, 0, 1)
    frames_out = lax.map(one_frame, jnp.arange(N_SEQ, dtype=jnp.int32))
    return frames_out.reshape(N_SEQ * frame_tokens, H * HD)
```

```python
import functools
import math

import jax
import jax.numpy as jnp
import numpy as np
from jax import lax
from jax.experimental import pallas as pl
from jax.experimental.pallas import tpu as pltpu
from jax.sharding import PartitionSpec as P

H = 48
HD = 128
TILE = 128
HT = 4
WT = 2
TILES = HT * WT
SLOTS = H // TILES
FRAMES = 3
NEG = -1e30
LOG2_SCALE = math.log2(math.e) / math.sqrt(HD)
MESH = pl.DeviceIdType.MESH
HALO_CHOICES = (3, 4, 6)


def power(exponent):
    return jnp.where(exponent > 0, 2.0, jnp.where(exponent < 0, 0.5, 1.0)).astype(jnp.float32)


def bytes_of(ref, sem):
    return pltpu.make_async_copy(ref, ref, sem)


def attend(q_ref, kv_ref, score_refs, write, table, slot, first_frame):
    frames = kv_ref.shape[0]

    def biases(row):
        rows = [table[slot, row * HT + r] for r in range(HT)]
        columns = [table[slot, HT * HT + c] for c in range(WT)]
        beside = [table[slot, HT * HT + WT + first_frame + f] for f in range(frames)]
        return lambda f, t, u: rows[t // WT] + columns[abs(t % WT - u)] + beside[f]

    def score(row, s_ref):
        bias = biases(row)
        queries = q_ref[pl.ds(row * WT, WT)].reshape(WT * TILE, HD)
        peak = [None] * WT
        for f in range(frames):
            for t in range(0, TILES, WT):
                keys = kv_ref[f, t : t + WT, 0].reshape(WT * TILE, HD)
                s = lax.dot_general(
                    keys, queries, (((1,), (1,)), ((), ())), preferred_element_type=jnp.float32
                )
                base = (f * TILES + t) * TILE
                s_ref[base : base + WT * TILE, :] = s
                for j in range(WT):
                    for u in range(WT):
                        block = s[j * TILE : (j + 1) * TILE, u * TILE : (u + 1) * TILE]
                        top = jnp.max(block.reshape(TILE // 8, 8, TILE), axis=0) + bias(f, t + j, u)
                        peak[u] = top if peak[u] is None else jnp.maximum(peak[u], top)
        return [jnp.max(p, axis=0, keepdims=True) * LOG2_SCALE for p in peak]

    def combine(row, s_ref, peak):
        bias = biases(row)
        ones = jnp.ones((16, WT * TILE), jnp.bfloat16)
        total = None
        for f in range(frames):
            for t in range(0, TILES, WT):
                base = (f * TILES + t) * TILE
                columns = []
                for u in range(WT):
                    parts = []
                    for j in range(WT):
                        s = s_ref[base + j * TILE : base + (j + 1) * TILE, u * TILE : (u + 1) * TILE]
                        shift = bias(f, t + j, u) - peak[u]
                        parts.append(jnp.exp2(s * LOG2_SCALE + shift).astype(jnp.bfloat16))
                    columns.append(jnp.concatenate(parts, axis=0))
                weights = jnp.concatenate(columns, axis=1)
                values = jnp.concatenate([kv_ref[f, t + j, 1] for j in range(WT)], axis=1)
                values = jnp.concatenate([values, ones], axis=0)
                part = jnp.dot(values, weights, preferred_element_type=jnp.float32)
                total = part if total is None else total + part
        out = total[:HD] * (1.0 / total[HD : HD + 1])
        for u in range(WT):
            write(row * WT + u, out[:, u * TILE : (u + 1) * TILE].T.astype(jnp.bfloat16))

    def rows(i, carry):
        at = [i * 2 + j for j in range(2)]
        peaks = [score(r, s_ref) for r, s_ref in zip(at, score_refs)]
        for r, s_ref, peak in zip(at, score_refs, peaks):
            combine(r, s_ref, peak)
        return carry

    lax.fori_loop(0, HT // 2, rows, 0)


def exchange_kernel(
    halo, frame_total,
    table, kv_stage, q_stage,
    out,
    kv_wide, kv_near, q_near, o_stage, scores_a, scores_b,
    kv_send, kv_recv, q_send, q_recv, halo_send, halo_recv, o_send, o_recv, own_sem,
):
    me = lax.axis_index("head")
    seq = lax.axis_index("seq")
    later = lax.rem(seq + 1, frame_total)
    earlier = lax.rem(seq + frame_total - 1, frame_total)

    def peer(d):
        return lax.rem(me + d, TILES)

    barrier = pltpu.get_barrier_semaphore()
    for d in range(1, TILES):
        pl.semaphore_signal(barrier, inc=1, device_id=(seq, peer(d)), device_id_type=MESH)
    for frame in (later, earlier):
        pl.semaphore_signal(barrier, inc=1, device_id=(frame, me), device_id_type=MESH)
    pl.semaphore_wait(barrier, TILES - 1 + 2)

    def send_kv(s, tile_at):
        for d in range(1, TILES):
            group = peer(d)
            pltpu.make_async_remote_copy(
                src_ref=kv_stage.at[s, group],
                dst_ref=tile_at(s, me),
                send_sem=kv_send.at[s],
                recv_sem=kv_recv.at[s],
                device_id=(seq, group),
                device_id_type=MESH,
            ).start()
        pltpu.make_async_copy(kv_stage.at[s, me], tile_at(s, me), own_sem.at[0, s]).start()

    def send_q(s):
        for d in range(1, TILES):
            group = peer(d)
            pltpu.make_async_remote_copy(
                src_ref=q_stage.at[s, group],
                dst_ref=q_near.at[s, me],
                send_sem=q_send.at[s],
                recv_sem=q_recv.at[s],
                device_id=(seq, group),
                device_id_type=MESH,
            ).start()
        pltpu.make_async_copy(q_stage.at[s, me], q_near.at[s, me], own_sem.at[1, s]).start()

    def wide_tile(s, t):
        return kv_wide.at[s, 1, t]

    def near_tile(s, t):
        return kv_near.at[s - halo, 0, t]

    def halo_copies(s):
        return [
            pltpu.make_async_remote_copy(
                src_ref=kv_wide.at[s, 1],
                dst_ref=kv_wide.at[s, 2 * side],
                send_sem=halo_send.at[s, side],
                recv_sem=halo_recv.at[s, side],
                device_id=(frame, me),
                device_id_type=MESH,
            )
            for side, frame in enumerate((later, earlier))
        ]

    def start_wide_kv(s, carry):
        send_kv(s, wide_tile)
        return carry

    def start_near_kv(s, carry):
        send_kv(s, near_tile)
        return carry

    def start_q(s, carry):
        send_q(s)
        return carry

    def forward(s, carry):
        bytes_of(kv_wide.at[s, 1, pl.ds(0, TILES - 1)], kv_recv.at[s]).wait()
        pltpu.make_async_copy(kv_stage.at[s, me], wide_tile(s, me), own_sem.at[0, s]).wait()
        for copy in halo_copies(s):
            copy.start()
        return carry

    lax.fori_loop(0, halo, start_wide_kv, 0)
    lax.fori_loop(0, halo, start_q, 0)
    if halo < SLOTS:
        lax.fori_loop(halo, SLOTS, start_near_kv, 0)
        lax.fori_loop(halo, SLOTS, start_q, 0)
    lax.fori_loop(0, halo, forward, 0)

    def attend_slot(s, kv_ref, first_frame):
        bytes_of(q_near.at[s, pl.ds(0, TILES - 1)], q_recv.at[s]).wait()
        pltpu.make_async_copy(q_stage.at[s, me], q_near.at[s, me], own_sem.at[1, s]).wait()

        def write(t, tile):
            o_stage[s, t] = tile

        attend(q_near.at[s], kv_ref, (scores_a, scores_b), write, table, s, first_frame)
        for d in range(1, TILES):
            group = peer(d)
            pltpu.make_async_remote_copy(
                src_ref=o_stage.at[s, group],
                dst_ref=out.at[s, me],
                send_sem=o_send.at[s],
                recv_sem=o_recv.at[s],
                device_id=(seq, group),
                device_id_type=MESH,
            ).start()
        pltpu.make_async_copy(o_stage.at[s, me], out.at[s, me], own_sem.at[2, s]).start()

    def wide_slot(s, carry):
        for copy in halo_copies(s):
            copy.wait_recv()
        attend_slot(s, kv_wide.at[s], 0)
        return carry

    def near_slot(s, carry):
        bytes_of(kv_near.at[s - halo, 0, pl.ds(0, TILES - 1)], kv_recv.at[s]).wait()
        pltpu.make_async_copy(kv_stage.at[s, me], near_tile(s, me), own_sem.at[0, s]).wait()
        attend_slot(s, kv_near.at[s - halo], 1)
        return carry

    lax.fori_loop(0, halo, wide_slot, 0)
    if halo < SLOTS:
        lax.fori_loop(halo, SLOTS, near_slot, 0)

    def finish(s, carry):
        bytes_of(kv_stage.at[s, pl.ds(0, TILES - 1)], kv_send.at[s]).wait()
        bytes_of(q_stage.at[s, pl.ds(0, TILES - 1)], q_send.at[s]).wait()
        pltpu.make_async_copy(o_stage.at[s, me], out.at[s, me], own_sem.at[2, s]).wait()
        bytes_of(o_stage.at[s, pl.ds(0, TILES - 1)], o_send.at[s]).wait()
        bytes_of(out.at[s, pl.ds(0, TILES - 1)], o_recv.at[s]).wait()
        return carry

    def finish_halo(s, carry):
        for copy in halo_copies(s):
            copy.wait_send()
        return carry

    lax.fori_loop(0, halo, finish_halo, 0)
    lax.fori_loop(0, SLOTS, finish, 0)


def prepare_kernel(order, q_exp, k_exp, v_exp, q_data, k_data, v_data, kv_out, q_out):
    slot = pl.program_id(0)
    for group in range(TILES):
        head = order[slot * TILES + group]
        columns = pl.ds(pl.multiple_of(head * HD, HD), HD)

        def scaled(ref, exps):
            return (ref[:, columns].astype(jnp.float32) * power(exps[0, head])).astype(jnp.bfloat16)

        kv_out[0, group, 0] = scaled(k_data, k_exp)
        kv_out[0, group, 1] = scaled(v_data, v_exp).T
        q_out[0, group] = scaled(q_data, q_exp)


def prepare(order, q_exp, k_exp, v_exp, q_data, k_data, v_data):
    smem = pl.BlockSpec(memory_space=pltpu.SMEM)
    whole = pl.BlockSpec((TILE, H * HD), lambda i: (0, 0))
    return pl.pallas_call(
        prepare_kernel,
        out_shape=(
            jax.ShapeDtypeStruct((SLOTS, TILES, 2, TILE, HD), jnp.bfloat16),
            jax.ShapeDtypeStruct((SLOTS, TILES, TILE, HD), jnp.bfloat16),
        ),
        grid=(SLOTS,),
        in_specs=[smem] * 4 + [whole] * 3,
        out_specs=(
            pl.BlockSpec((1, TILES, 2, TILE, HD), lambda i: (i, 0, 0, 0, 0)),
            pl.BlockSpec((1, TILES, TILE, HD), lambda i: (i, 0, 0, 0)),
        ),
        compiler_params=pltpu.CompilerParams(vmem_limit_bytes=32 << 20),
        name="prepare",
    )(order, q_exp, k_exp, v_exp, q_data, k_data, v_data)


def exchange(halo, collective_id, frame_total, operands):
    near = max(SLOTS - halo, 1)
    smem = pl.BlockSpec(memory_space=pltpu.SMEM)
    hbm = pl.BlockSpec(memory_space=pl.ANY)
    bf16 = jnp.bfloat16
    tile = (TILE, HD)
    return pl.pallas_call(
        functools.partial(exchange_kernel, halo, frame_total),
        out_shape=jax.ShapeDtypeStruct((SLOTS, TILES) + tile, bf16),
        in_specs=[smem] + [hbm] * 2,
        out_specs=hbm,
        scratch_shapes=[
            pltpu.VMEM((halo, FRAMES, TILES, 2) + tile, bf16),
            pltpu.VMEM((near, 1, TILES, 2) + tile, bf16),
            pltpu.VMEM((SLOTS, TILES) + tile, bf16),
            pltpu.VMEM((SLOTS, TILES) + tile, bf16),
            pltpu.VMEM((FRAMES * TILES * TILE, WT * TILE), jnp.float32),
            pltpu.VMEM((FRAMES * TILES * TILE, WT * TILE), jnp.float32),
            pltpu.SemaphoreType.DMA((SLOTS,)),
            pltpu.SemaphoreType.DMA((SLOTS,)),
            pltpu.SemaphoreType.DMA((SLOTS,)),
            pltpu.SemaphoreType.DMA((SLOTS,)),
            pltpu.SemaphoreType.DMA((halo, 2)),
            pltpu.SemaphoreType.DMA((halo, 2)),
            pltpu.SemaphoreType.DMA((SLOTS,)),
            pltpu.SemaphoreType.DMA((SLOTS,)),
            pltpu.SemaphoreType.DMA((3, SLOTS)),
        ],
        compiler_params=pltpu.CompilerParams(
            collective_id=collective_id, has_side_effects=True, vmem_limit_bytes=50 << 20
        ),
        name=f"exchange_{halo}",
    )(*operands)


def restore_kernel(place, tiles, out):
    heads = out.shape[1] // HD
    for i in range(heads):
        out[:, i * HD : (i + 1) * HD] = tiles[place[pl.program_id(0) * heads + i]]


def restore(place, tiles):
    blocks = 4
    return pl.pallas_call(
        restore_kernel,
        out_shape=jax.ShapeDtypeStruct((TILE, H * HD), jnp.bfloat16),
        grid=(blocks,),
        in_specs=[
            pl.BlockSpec(memory_space=pltpu.SMEM),
            pl.BlockSpec((H, TILE, HD), lambda i: (0, 0, 0)),
        ],
        out_specs=pl.BlockSpec((TILE, H * HD // blocks), lambda i: (0, i)),
        compiler_params=pltpu.CompilerParams(vmem_limit_bytes=16 << 20),
        name="restore",
    )(place, tiles)


def on_device(frame_total, q_data, k_data, v_data, q_exp, k_exp, v_exp, extents):
    index = jnp.arange(H, dtype=jnp.int32)
    sort_key = (1 - extents[:, 0]) * H + index
    place = jnp.sum((sort_key[None, :] < sort_key[:, None]).astype(jnp.int32), axis=1)
    order = jnp.sum(jnp.where(place[None, :] == index[:, None], index[None, :], 0), axis=1)
    reaching = jnp.sum((extents[:, 0] > 0).astype(jnp.int32))
    choice = sum((reaching > n * TILES).astype(jnp.int32) for n in HALO_CHOICES[:-1])
    own = place[None, :] == jnp.arange(SLOTS)[:, None] * TILES + lax.axis_index("head")
    extent = jnp.sum(jnp.where(own[:, :, None], extents[None], 0), axis=1)
    seq = lax.axis_index("seq")
    row = np.arange(HT)
    need = jnp.concatenate(
        [
            jnp.broadcast_to(extent[:, 1:2], (SLOTS, HT * HT)),
            jnp.broadcast_to(extent[:, 2:3], (SLOTS, WT)),
            jnp.broadcast_to(extent[:, 0:1], (SLOTS, FRAMES)),
        ],
        axis=1,
    )
    apart = np.concatenate(
        [np.abs(row[:, None] - row[None]).ravel(), np.arange(WT), np.abs(np.arange(FRAMES) - 1)]
    )
    step = np.concatenate([np.zeros(HT * HT + WT, int), np.arange(FRAMES) - 1])
    inside = (seq + step >= 0) & (seq + step < frame_total)
    table = jnp.where((need >= apart[None]) & inside[None], 0.0, NEG).astype(jnp.float32)
    kv_stage, q_stage = prepare(order, q_exp, k_exp, v_exp, q_data, k_data, v_data)
    operands = (table, kv_stage, q_stage)
    branches = [
        functools.partial(lambda n, i, *ops: exchange(n, i, frame_total, ops), n, i)
        for i, n in enumerate(HALO_CHOICES)
    ]
    tiles = lax.switch(choice, branches, *operands)
    return restore(place, tiles.reshape(H, TILE, HD))


def solution(mesh):
    rows = P(("seq", "head"), None)
    return jax.shard_map(
        functools.partial(on_device, mesh.shape["seq"]),
        mesh=mesh,
        in_specs=(rows,) * 6 + (P(),),
        out_specs=rows,
        check_vma=False,
    )
```

```python
import functools
import math

import jax
import jax.numpy as jnp
from jax import lax
from jax.experimental import pallas as pl
from jax.experimental.pallas import tpu as pltpu
from jax.sharding import PartitionSpec as P

H = 48
HD = 128
TILE = 128
HT = 4
WT = 2
TILES = HT * WT
SLOTS = H // TILES
FRAMES = 3
NEG = -1e30
LOG2_SCALE = math.log2(math.e) / math.sqrt(HD)
MESH = pl.DeviceIdType.MESH
PLANS = ((5, 2), (5, 3), (5, 5), (6, 4), (6, 6))
TABLE = (SLOTS + TILES, HT * HT + WT + FRAMES)


def power(exponent):
    return jnp.where(exponent > 0, 2.0, jnp.where(exponent < 0, 0.5, 1.0)).astype(jnp.float32)


def bytes_of(ref, sem):
    return pltpu.make_async_copy(ref, ref, sem)


def block_max(s):
    return jnp.max(s.reshape(s.shape[0] // 8, 8, s.shape[1]), axis=0)


def attend(q_ref, kv_ref, score_refs, write, table, slot, first_frame):
    frames = kv_ref.shape[0]

    def biases(row):
        rows = [table[slot, row * HT + r] for r in range(HT)]
        columns = [table[slot, HT * HT + c] for c in range(WT)]
        beside = [table[slot, HT * HT + WT + first_frame + f] for f in range(frames)]
        return lambda f, t, u: rows[t // WT] + columns[abs(t % WT - u)] + beside[f]

    def score(row, s_ref):
        bias = biases(row)
        queries = q_ref[pl.ds(row * WT, WT)].reshape(WT * TILE, HD)
        peak = [None] * WT
        for f in range(frames):
            for t in range(0, TILES, WT):
                keys = kv_ref[f, t : t + WT, 0].reshape(WT * TILE, HD)
                s = lax.dot_general(
                    keys, queries, (((1,), (1,)), ((), ())), preferred_element_type=jnp.float32
                )
                base = (f * TILES + t) * TILE
                s_ref[base : base + WT * TILE, :] = s
                for j in range(WT):
                    for u in range(WT):
                        block = s[j * TILE : (j + 1) * TILE, u * TILE : (u + 1) * TILE]
                        top = block_max(block) + bias(f, t + j, u)
                        peak[u] = top if peak[u] is None else jnp.maximum(peak[u], top)
        return [jnp.max(p, axis=0, keepdims=True) * LOG2_SCALE for p in peak]

    def combine(row, s_ref, peak):
        bias = biases(row)
        ones = jnp.ones((16, WT * TILE), jnp.bfloat16)
        total = None
        for f in range(frames):
            for t in range(0, TILES, WT):
                base = (f * TILES + t) * TILE
                columns = []
                for u in range(WT):
                    parts = []
                    for j in range(WT):
                        s = s_ref[base + j * TILE : base + (j + 1) * TILE, u * TILE : (u + 1) * TILE]
                        shift = bias(f, t + j, u) - peak[u]
                        parts.append(jnp.exp2(s * LOG2_SCALE + shift).astype(jnp.bfloat16))
                    columns.append(jnp.concatenate(parts, axis=0))
                weights = jnp.concatenate(columns, axis=1)
                values = jnp.concatenate([kv_ref[f, t + j, 1] for j in range(WT)], axis=1)
                values = jnp.concatenate([values, ones], axis=0)
                part = jnp.dot(values, weights, preferred_element_type=jnp.float32)
                total = part if total is None else total + part
        out = total[:HD] * (1.0 / total[HD : HD + 1])
        for u in range(WT):
            write(row * WT + u, out[:, u * TILE : (u + 1) * TILE].T.astype(jnp.bfloat16))

    def rows(i, carry):
        at = [i * 2 + j for j in range(2)]
        peaks = [score(r, s_ref) for r, s_ref in zip(at, score_refs)]
        for r, s_ref, peak in zip(at, score_refs, peaks):
            combine(r, s_ref, peak)
        return carry

    lax.fori_loop(0, HT // 2, rows, 0)


def attend_row(queries, kv_ref, head, table):
    frames = kv_ref.shape[0]
    row = SLOTS + head
    columns = [table[row, c] for c in range(WT)]
    beside = [table[row, WT + f] for f in range(frames)]
    scores = []
    peak = None
    for f in range(frames):
        for c in range(WT):
            keys = kv_ref[f, c, head, 0]
            s = lax.dot_general(
                keys, queries, (((1,), (1,)), ((), ())), preferred_element_type=jnp.float32
            )
            scores.append(s)
            top = block_max(s) + (columns[c] + beside[f])
            peak = top if peak is None else jnp.maximum(peak, top)
    peak = jnp.max(peak, axis=0, keepdims=True) * LOG2_SCALE
    ones = jnp.ones((16, WT * TILE), jnp.bfloat16)
    total = None
    for f in range(frames):
        weights = jnp.concatenate(
            [
                jnp.exp2(scores[f * WT + c] * LOG2_SCALE + (columns[c] + beside[f] - peak))
                for c in range(WT)
            ],
            axis=0,
        ).astype(jnp.bfloat16)
        values = jnp.concatenate([kv_ref[f, c, head, 1] for c in range(WT)], axis=1)
        values = jnp.concatenate([values, ones], axis=0)
        part = jnp.dot(values, weights, preferred_element_type=jnp.float32)
        total = part if total is None else total + part
    return (total[:HD] * (1.0 / total[HD : HD + 1])).T.astype(jnp.bfloat16)


def exchange_kernel(
    slots, halo, frame_total,
    table, kv_stage, q_stage,
    out,
    kv_wide, kv_near, kv_row, q_near, o_stage, scores_a, scores_b,
    kv_send, kv_recv, q_send, q_recv, halo_send, halo_recv, o_send, o_recv, own_sem,
    row_send, row_recv, side_send, side_recv,
):
    by_row = slots < SLOTS
    last = SLOTS - 1
    me = lax.axis_index("head")
    seq = lax.axis_index("seq")
    later = lax.rem(seq + 1, frame_total)
    earlier = lax.rem(seq + frame_total - 1, frame_total)

    def peer(d):
        return lax.rem(me + d, TILES)

    barrier = pltpu.get_barrier_semaphore()
    for d in range(1, TILES):
        pl.semaphore_signal(barrier, inc=1, device_id=(seq, peer(d)), device_id_type=MESH)
    for frame in (later, earlier):
        pl.semaphore_signal(barrier, inc=1, device_id=(frame, me), device_id_type=MESH)
    pl.semaphore_wait(barrier, TILES - 1 + 2)

    def send_kv(s, tile_at):
        for d in range(1, TILES):
            group = peer(d)
            pltpu.make_async_remote_copy(
                src_ref=kv_stage.at[s, group],
                dst_ref=tile_at(s, me),
                send_sem=kv_send.at[s],
                recv_sem=kv_recv.at[s],
                device_id=(seq, group),
                device_id_type=MESH,
            ).start()
        pltpu.make_async_copy(kv_stage.at[s, me], tile_at(s, me), own_sem.at[0, s]).start()

    def send_q(s):
        for d in range(1, TILES):
            group = peer(d)
            pltpu.make_async_remote_copy(
                src_ref=q_stage.at[s, group],
                dst_ref=q_near.at[s, me],
                send_sem=q_send.at[s],
                recv_sem=q_recv.at[s],
                device_id=(seq, group),
                device_id_type=MESH,
            ).start()
        pltpu.make_async_copy(q_stage.at[s, me], q_near.at[s, me], own_sem.at[1, s]).start()

    def wide_tile(s, t):
        return kv_wide.at[s, 1, t]

    def near_tile(s, t):
        return kv_near.at[s - halo, 0, t]

    def halo_copies(s):
        return [
            pltpu.make_async_remote_copy(
                src_ref=kv_wide.at[s, 1],
                dst_ref=kv_wide.at[s, 2 * side],
                send_sem=halo_send.at[s, side],
                recv_sem=halo_recv.at[s, side],
                device_id=(frame, me),
                device_id_type=MESH,
            )
            for side, frame in enumerate((later, earlier))
        ]

    column = lax.rem(me, WT)
    sibling = me + 1 - 2 * column

    def to_sibling(source, f):
        return pltpu.make_async_remote_copy(
            src_ref=source,
            dst_ref=kv_row.at[f, column],
            send_sem=side_send.at[f],
            recv_sem=side_recv.at[f],
            device_id=(seq, sibling),
            device_id_type=MESH,
        )

    def row_halo():
        return [
            pltpu.make_async_remote_copy(
                src_ref=kv_stage.at[last],
                dst_ref=kv_row.at[2 * side, column],
                send_sem=row_send.at[side],
                recv_sem=row_recv.at[side],
                device_id=(frame, me),
                device_id_type=MESH,
            )
            for side, frame in enumerate((later, earlier))
        ]

    def own_row():
        return [
            pltpu.make_async_copy(kv_stage.at[last], kv_row.at[1, column], own_sem.at[0, last]),
            pltpu.make_async_copy(q_stage.at[last], q_near.at[last], own_sem.at[1, last]),
        ]

    def start_wide_kv(s, carry):
        send_kv(s, wide_tile)
        return carry

    def start_near_kv(s, carry):
        send_kv(s, near_tile)
        send_q(s)
        return carry

    def start_q(s, carry):
        send_q(s)
        return carry

    def forward(s, carry):
        bytes_of(kv_wide.at[s, 1, pl.ds(0, TILES - 1)], kv_recv.at[s]).wait()
        pltpu.make_async_copy(kv_stage.at[s, me], wide_tile(s, me), own_sem.at[0, s]).wait()
        for copy in halo_copies(s):
            copy.start()
        return carry

    send_kv(0, wide_tile)
    if by_row:
        for copy in row_halo():
            copy.start()
        to_sibling(kv_stage.at[last], 1).start()
        for copy in own_row():
            copy.start()
    lax.fori_loop(1, halo, start_wide_kv, 0)
    lax.fori_loop(0, halo, start_q, 0)
    if halo < slots:
        lax.fori_loop(halo, slots, start_near_kv, 0)
    lax.fori_loop(0, 2, forward, 0)
    if by_row:
        for side, copy in enumerate(row_halo()):
            copy.wait_recv()
            to_sibling(kv_row.at[2 * side, column], 2 * side).start()
    if halo > 2:
        lax.fori_loop(2, halo, forward, 0)

    if by_row:
        for copy in own_row():
            copy.wait()
        for f, source in enumerate((kv_row.at[0, column], kv_stage.at[last], kv_row.at[2, column])):
            to_sibling(source, f).wait_recv()

        def row_heads(i, carry):
            for j in range(2):
                head = i * 2 + j
                o_stage[last, head] = attend_row(q_near[last, head], kv_row, head, table)
            return carry

        lax.fori_loop(0, TILES // 2, row_heads, 0)
        pltpu.make_async_copy(o_stage.at[last], out.at[last], own_sem.at[2, last]).start()

    def attend_slot(s, kv_ref, first_frame):
        bytes_of(q_near.at[s, pl.ds(0, TILES - 1)], q_recv.at[s]).wait()
        pltpu.make_async_copy(q_stage.at[s, me], q_near.at[s, me], own_sem.at[1, s]).wait()

        def write(t, tile):
            o_stage[s, t] = tile

        attend(q_near.at[s], kv_ref, (scores_a, scores_b), write, table, s, first_frame)
        for d in range(1, TILES):
            group = peer(d)
            pltpu.make_async_remote_copy(
                src_ref=o_stage.at[s, group],
                dst_ref=out.at[s, me],
                send_sem=o_send.at[s],
                recv_sem=o_recv.at[s],
                device_id=(seq, group),
                device_id_type=MESH,
            ).start()
        pltpu.make_async_copy(o_stage.at[s, me], out.at[s, me], own_sem.at[2, s]).start()

    def wide_slot(s, carry):
        for copy in halo_copies(s):
            copy.wait_recv()
        attend_slot(s, kv_wide.at[s], 0)
        return carry

    def near_slot(s, carry):
        bytes_of(kv_near.at[s - halo, 0, pl.ds(0, TILES - 1)], kv_recv.at[s]).wait()
        pltpu.make_async_copy(kv_stage.at[s, me], near_tile(s, me), own_sem.at[0, s]).wait()
        attend_slot(s, kv_near.at[s - halo], 1)
        return carry

    near = slots - halo
    first = max(halo - near, 0)

    def pair(j, carry):
        near_slot(halo + j, 0)
        wide_slot(first + j, 0)
        return carry

    if first:
        lax.fori_loop(0, first, wide_slot, 0)
    if near:
        lax.fori_loop(0, min(near, halo), pair, 0)
    if near > halo:
        lax.fori_loop(halo + halo, slots, near_slot, 0)

    def finish(s, carry):
        bytes_of(kv_stage.at[s, pl.ds(0, TILES - 1)], kv_send.at[s]).wait()
        bytes_of(q_stage.at[s, pl.ds(0, TILES - 1)], q_send.at[s]).wait()
        pltpu.make_async_copy(o_stage.at[s, me], out.at[s, me], own_sem.at[2, s]).wait()
        bytes_of(o_stage.at[s, pl.ds(0, TILES - 1)], o_send.at[s]).wait()
        bytes_of(out.at[s, pl.ds(0, TILES - 1)], o_recv.at[s]).wait()
        return carry

    def finish_halo(s, carry):
        for copy in halo_copies(s):
            copy.wait_send()
        return carry

    lax.fori_loop(0, halo, finish_halo, 0)
    if by_row:
        for copy in row_halo():
            copy.wait_send()
        for f, source in enumerate((kv_row.at[0, column], kv_stage.at[last], kv_row.at[2, column])):
            to_sibling(source, f).wait_send()
        pltpu.make_async_copy(o_stage.at[last], out.at[last], own_sem.at[2, last]).wait()
    lax.fori_loop(0, slots, finish, 0)


def prepare_kernel(
    frame_total,
    extents, q_exp, k_exp, v_exp, q_data, k_data, v_data,
    table, place, plan, kv_out, q_out,
    order, q_in, k_in, v_in, kv_stage, q_stage, in_sem, out_sem,
):
    loads = [
        pltpu.make_async_copy(src, dst, in_sem.at[i])
        for i, (src, dst) in enumerate(((k_data, k_in), (v_data, v_in), (q_data, q_in)))
    ]
    for load in loads:
        load.start()

    zero = jnp.int32(0)
    reach = [(extents[0, h] >= 1).astype(jnp.int32) for h in range(H)]
    flat = [(extents[1, h] <= 0).astype(jnp.int32) for h in range(H)]
    reaching = sum(reach, zero)
    flat_reaching = sum((r * f for r, f in zip(reach, flat)), zero)
    by_row = (sum(flat, zero) >= TILES).astype(jnp.int32)
    row_reaching = by_row * jnp.minimum(flat_reaching, TILES)
    rest_reaching = reaching - row_reaching
    next_row_reach, next_row_rest = zero, row_reaching
    next_reach, next_rest = zero, rest_reaching
    for h in range(H):
        row_index = jnp.where(reach[h] > 0, next_row_reach, next_row_rest)
        in_row = by_row * flat[h] * (row_index < TILES).astype(jnp.int32)
        outside = 1 - in_row
        spot = jnp.where(
            in_row > 0,
            H - TILES + row_index,
            jnp.where(reach[h] > 0, next_reach, next_rest),
        )
        next_row_reach += in_row * reach[h]
        next_row_rest += in_row * (1 - reach[h])
        next_reach += outside * reach[h]
        next_rest += outside * (1 - reach[h])
        order[spot] = h
        place[h] = spot
    wide = [rest_reaching > n * TILES for n in (2, 3, 4)]
    with_row = wide[0].astype(jnp.int32) + wide[1].astype(jnp.int32)
    plan[0] = jnp.where(by_row > 0, with_row, 3 + wide[2].astype(jnp.int32))

    me = lax.axis_index("head")
    seq = lax.axis_index("seq")
    column = lax.rem(me, WT)

    def within(condition):
        return jnp.where(condition, 0.0, NEG).astype(jnp.float32)

    def beside(head, f):
        inside = (seq + f - 1 >= 0) & (seq + f - 1 < frame_total)
        return within((extents[0, head] >= abs(f - 1)) & inside)

    for s in range(SLOTS):
        head = order[s * TILES + me]
        for r in range(HT):
            for t in range(HT):
                table[s, r * HT + t] = within(extents[1, head] >= abs(r - t))
        for c in range(WT):
            table[s, HT * HT + c] = within(extents[2, head] >= c)
        for f in range(FRAMES):
            table[s, HT * HT + WT + f] = beside(head, f)
    for i in range(TILES):
        head = order[H - TILES + i]
        for c in range(WT):
            table[SLOTS + i, c] = within(extents[2, head] >= jnp.abs(column - c))
        for f in range(FRAMES):
            table[SLOTS + i, WT + f] = beside(head, f)

    def scaled(ref, exps, head):
        columns = pl.ds(pl.multiple_of(head * HD, HD), HD)
        return (ref[:, columns].astype(jnp.float32) * power(exps[0, head])).astype(jnp.bfloat16)

    def kv_copy(s, which):
        return pltpu.make_async_copy(
            kv_stage.at[s, :, which], kv_out.at[s, :, which], out_sem.at[which, s]
        )

    def q_copy(s):
        return pltpu.make_async_copy(q_stage.at[s], q_out.at[s], out_sem.at[2, s])

    def stage_keys(s, carry):
        for g in range(TILES):
            kv_stage[s, g, 0] = scaled(k_in, k_exp, order[s * TILES + g])
        kv_copy(s, 0).start()
        return carry

    def stage_values(s, carry):
        for g in range(TILES):
            kv_stage[s, g, 1] = scaled(v_in, v_exp, order[s * TILES + g]).T
        kv_copy(s, 1).start()
        return carry

    def stage_queries(s, carry):
        for g in range(TILES):
            q_stage[s, g] = scaled(q_in, q_exp, order[s * TILES + g])
        q_copy(s).start()
        return carry

    for load, stage in zip(loads, (stage_keys, stage_values, stage_queries)):
        load.wait()
        lax.fori_loop(0, SLOTS, stage, 0)
    for s in range(SLOTS):
        kv_copy(s, 0).wait()
        kv_copy(s, 1).wait()
        q_copy(s).wait()


def prepare(frame_total, extents, q_exp, k_exp, v_exp, q_data, k_data, v_data):
    smem = pl.BlockSpec(memory_space=pltpu.SMEM)
    hbm = pl.BlockSpec(memory_space=pl.ANY)
    bf16 = jnp.bfloat16
    kv = (SLOTS, TILES, 2, TILE, HD)
    q = (SLOTS, TILES, TILE, HD)
    whole = pltpu.VMEM((TILE, H * HD), bf16)
    return pl.pallas_call(
        functools.partial(prepare_kernel, frame_total),
        out_shape=(
            jax.ShapeDtypeStruct(TABLE, jnp.float32),
            jax.ShapeDtypeStruct((H,), jnp.int32),
            jax.ShapeDtypeStruct((1,), jnp.int32),
            jax.ShapeDtypeStruct(kv, bf16),
            jax.ShapeDtypeStruct(q, bf16),
        ),
        in_specs=[smem] * 4 + [hbm] * 3,
        out_specs=(smem, smem, smem, hbm, hbm),
        scratch_shapes=[
            pltpu.SMEM((H,), jnp.int32),
            whole, whole, whole,
            pltpu.VMEM(kv, bf16),
            pltpu.VMEM(q, bf16),
            pltpu.SemaphoreType.DMA((3,)),
            pltpu.SemaphoreType.DMA((3, SLOTS)),
        ],
        compiler_params=pltpu.CompilerParams(vmem_limit_bytes=60 << 20),
        name="prepare",
    )(extents, q_exp, k_exp, v_exp, q_data, k_data, v_data)


def exchange(slots, halo, collective_id, frame_total, operands):
    near = max(slots - halo, 1)
    rows = TILES if slots < SLOTS else 1
    smem = pl.BlockSpec(memory_space=pltpu.SMEM)
    hbm = pl.BlockSpec(memory_space=pl.ANY)
    bf16 = jnp.bfloat16
    tile = (TILE, HD)
    return pl.pallas_call(
        functools.partial(exchange_kernel, slots, halo, frame_total),
        out_shape=jax.ShapeDtypeStruct((SLOTS, TILES) + tile, bf16),
        in_specs=[smem] + [hbm] * 2,
        out_specs=hbm,
        scratch_shapes=[
            pltpu.VMEM((halo, FRAMES, TILES, 2) + tile, bf16),
            pltpu.VMEM((near, 1, TILES, 2) + tile, bf16),
            pltpu.VMEM((FRAMES, WT, rows, 2) + tile, bf16),
            pltpu.VMEM((SLOTS, TILES) + tile, bf16),
            pltpu.VMEM((SLOTS, TILES) + tile, bf16),
            pltpu.VMEM((FRAMES * TILES * TILE, WT * TILE), jnp.float32),
            pltpu.VMEM((FRAMES * TILES * TILE, WT * TILE), jnp.float32),
            pltpu.SemaphoreType.DMA((SLOTS,)),
            pltpu.SemaphoreType.DMA((SLOTS,)),
            pltpu.SemaphoreType.DMA((SLOTS,)),
            pltpu.SemaphoreType.DMA((SLOTS,)),
            pltpu.SemaphoreType.DMA((halo, 2)),
            pltpu.SemaphoreType.DMA((halo, 2)),
            pltpu.SemaphoreType.DMA((SLOTS,)),
            pltpu.SemaphoreType.DMA((SLOTS,)),
            pltpu.SemaphoreType.DMA((3, SLOTS)),
            pltpu.SemaphoreType.DMA((2,)),
            pltpu.SemaphoreType.DMA((2,)),
            pltpu.SemaphoreType.DMA((FRAMES,)),
            pltpu.SemaphoreType.DMA((FRAMES,)),
        ],
        compiler_params=pltpu.CompilerParams(
            collective_id=collective_id, has_side_effects=True, vmem_limit_bytes=60 << 20
        ),
        name=f"exchange_{slots}_{halo}",
    )(*operands)


def restore_kernel(place, tiles, out, sem):
    for h in range(H):
        pltpu.make_async_copy(tiles.at[place[h]], out.at[:, pl.ds(h * HD, HD)], sem).start()
    pltpu.make_async_copy(out, out, sem).wait()


def restore(place, tiles):
    hbm = pl.BlockSpec(memory_space=pl.ANY)
    return pl.pallas_call(
        restore_kernel,
        out_shape=jax.ShapeDtypeStruct((TILE, H * HD), jnp.bfloat16),
        in_specs=[pl.BlockSpec(memory_space=pltpu.SMEM), hbm],
        out_specs=hbm,
        scratch_shapes=[pltpu.SemaphoreType.DMA(())],
        compiler_params=pltpu.CompilerParams(vmem_limit_bytes=60 << 20),
        name="restore",
    )(place, tiles)


def on_device(frame_total, q_data, k_data, v_data, q_exp, k_exp, v_exp, extents):
    table, place, plan, kv_stage, q_stage = prepare(
        frame_total, extents.T, q_exp, k_exp, v_exp, q_data, k_data, v_data
    )
    branches = [
        functools.partial(lambda p, i, *ops: exchange(*p, i, frame_total, ops), p, i)
        for i, p in enumerate(PLANS)
    ]
    tiles = lax.switch(plan[0], branches, table, kv_stage, q_stage)
    return restore(place, tiles.reshape(H, TILE, HD))


def solution(mesh):
    rows = P(("seq", "head"), None)
    return jax.shard_map(
        functools.partial(on_device, mesh.shape["seq"]),
        mesh=mesh,
        in_specs=(rows,) * 6 + (P(),),
        out_specs=rows,
        check_vma=False,
    )
```

```python
import functools
import math

import jax
import jax.numpy as jnp
from jax import lax
from jax.experimental import pallas as pl
from jax.experimental.pallas import tpu as pltpu
from jax.sharding import PartitionSpec as P

H = 48
HD = 128
TILE = 128
HT = 4
WT = 2
TILES = HT * WT
HALF = TILES // 2
FRAMES = 3
NEG = -1e30
LOG2_SCALE = math.log2(math.e) / math.sqrt(HD)
MESH = pl.DeviceIdType.MESH

PLANS = ((9, 3), (10, 3), (12, 6))
ROW_HEADS = 12
ROW_REACH = 8

SLOTS = H // TILES
ENTRIES = HT * HT + WT + FRAMES
ROW_TABLE = SLOTS * ENTRIES
ROW_ENTRIES = WT + FRAMES
TABLE = ROW_TABLE + ROW_HEADS * ROW_ENTRIES


def bytes_of(ref, sem):
    return pltpu.make_async_copy(ref, ref, sem)


def block_max(s):
    return jnp.max(s.reshape(s.shape[0] // 8, 8, s.shape[1]), axis=0)


def attend(q_ref, kv_ref, score_refs, write, table, slot, first_frame):
    frames = kv_ref.shape[0]
    entry = slot * ENTRIES

    def biases(row):
        rows = [table[entry + row * HT + r] for r in range(HT)]
        columns = [table[entry + HT * HT + c] for c in range(WT)]
        beside = [table[entry + HT * HT + WT + first_frame + f] for f in range(frames)]
        return lambda f, t, u: rows[t // WT] + columns[abs(t % WT - u)] + beside[f]

    def score(row, s_ref):
        bias = biases(row)
        queries = q_ref[pl.ds(row * WT, WT)].reshape(WT * TILE, HD)
        peak = [None] * WT
        for f in range(frames):
            for t in range(0, TILES, WT):
                keys = kv_ref[f, t : t + WT, 0].reshape(WT * TILE, HD)
                s = lax.dot_general(
                    keys, queries, (((1,), (1,)), ((), ())), preferred_element_type=jnp.float32
                )
                base = (f * TILES + t) * TILE
                s_ref[base : base + WT * TILE, :] = s
                for j in range(WT):
                    for u in range(WT):
                        block = s[j * TILE : (j + 1) * TILE, u * TILE : (u + 1) * TILE]
                        top = block_max(block) + bias(f, t + j, u)
                        peak[u] = top if peak[u] is None else jnp.maximum(peak[u], top)
        return [jnp.max(p, axis=0, keepdims=True) * LOG2_SCALE for p in peak]

    def combine(row, s_ref, peak):
        bias = biases(row)
        ones = jnp.ones((16, WT * TILE), jnp.bfloat16)
        total = None
        for f in range(frames):
            for t in range(0, TILES, WT):
                base = (f * TILES + t) * TILE
                columns = []
                for u in range(WT):
                    parts = []
                    for j in range(WT):
                        s = s_ref[base + j * TILE : base + (j + 1) * TILE, u * TILE : (u + 1) * TILE]
                        shift = bias(f, t + j, u) - peak[u]
                        parts.append(jnp.exp2(s * LOG2_SCALE + shift).astype(jnp.bfloat16))
                    columns.append(jnp.concatenate(parts, axis=0))
                weights = jnp.concatenate(columns, axis=1)
                values = jnp.concatenate([kv_ref[f, t + j, 1] for j in range(WT)], axis=1)
                values = jnp.concatenate([values, ones], axis=0)
                part = jnp.dot(values, weights, preferred_element_type=jnp.float32)
                total = part if total is None else total + part
        out = total[:HD] * (1.0 / total[HD : HD + 1])
        for u in range(WT):
            write(row * WT + u, out[:, u * TILE : (u + 1) * TILE].T.astype(jnp.bfloat16))

    def rows(i, carry):
        at = [i * 2 + j for j in range(2)]
        peaks = [score(r, s_ref) for r, s_ref in zip(at, score_refs)]
        for r, s_ref, peak in zip(at, score_refs, peaks):
            combine(r, s_ref, peak)
        return carry

    lax.fori_loop(0, HT // 2, rows, 0)


def attend_row(queries, kv_ref, frames, head, table):
    entry = ROW_TABLE + head * ROW_ENTRIES
    columns = [table[entry + c] for c in range(WT)]
    blocks = [(f, c, columns[c] + table[entry + WT + f]) for f in frames for c in range(WT)]
    scores = []
    peak = None
    for f, c, bias in blocks:
        s = lax.dot_general(
            kv_ref[f, c, head, 0], queries, (((1,), (1,)), ((), ())), preferred_element_type=jnp.float32
        )
        scores.append(s)
        top = block_max(s) + bias
        peak = top if peak is None else jnp.maximum(peak, top)
    peak = jnp.max(peak, axis=0, keepdims=True) * LOG2_SCALE
    weights = jnp.concatenate(
        [jnp.exp2(s * LOG2_SCALE + (bias - peak)) for s, (_, _, bias) in zip(scores, blocks)], axis=0
    ).astype(jnp.bfloat16)
    values = jnp.concatenate([kv_ref[f, c, head, 1] for f, c, _ in blocks], axis=1)
    values = jnp.concatenate([values, jnp.ones((16, values.shape[1]), jnp.bfloat16)], axis=0)
    total = jnp.dot(values, weights, preferred_element_type=jnp.float32)
    return (total[:HD] * (1.0 / total[HD : HD + 1])).T.astype(jnp.bfloat16)


def exchange_kernel(
    halves, wide, frame_total,
    table_hbm, kv_stage, q_stage,
    out,
    table, kv_wide, kv_near, kv_row, q_near, q_row, o_stage, o_row, scores_a, scores_b,
    table_sem, kv_send, kv_recv, q_send, q_recv, halo_send, halo_recv, o_send, o_recv, own_sem,
    row_send, row_recv, side_send, side_recv, row_sem,
):
    full, half = halves // 2, halves % 2
    slots = full + half
    row_base = halves * HALF
    row_heads = H - row_base
    me = lax.axis_index("head")
    seq = lax.axis_index("seq")
    later = lax.rem(seq + 1, frame_total)
    earlier = lax.rem(seq + frame_total - 1, frame_total)
    column = lax.rem(me, WT)
    chip = me // WT
    sibling = me + 1 - 2 * column
    spot = column * HALF + chip

    table_load = pltpu.make_async_copy(table_hbm, table, table_sem.at[0])
    table_load.start()

    def peer(d):
        return lax.rem(me + d, TILES)

    barrier = pltpu.get_barrier_semaphore()
    for d in range(1, TILES):
        pl.semaphore_signal(barrier, inc=1, device_id=(seq, peer(d)), device_id_type=MESH)
    for frame in (later, earlier):
        pl.semaphore_signal(barrier, inc=1, device_id=(frame, me), device_id_type=MESH)
    pl.semaphore_wait(barrier, TILES - 1 + 2)

    def remote(src, dst, send, recv, frame, group):
        return pltpu.make_async_remote_copy(
            src_ref=src, dst_ref=dst, send_sem=send, recv_sem=recv,
            device_id=(frame, group), device_id_type=MESH,
        )

    def wide_tile(s, t):
        return kv_wide.at[s, 1, t]

    def near_tile(s, t):
        return kv_near.at[s - wide, 0, t]

    def send_kv_tile(s, place, tile_at, group):
        src = kv_stage.at[s * TILES + place]
        remote(src, tile_at(s, me), kv_send.at[s], kv_recv.at[s], seq, group).start()

    def send_q_tile(s, place, group):
        src = q_stage.at[s * TILES + place]
        remote(src, q_near.at[s, me], q_send.at[s], q_recv.at[s], seq, group).start()

    def own_kv(s, tile_at):
        return pltpu.make_async_copy(kv_stage.at[s * TILES + spot], tile_at(s, me), own_sem.at[0, s])

    def own_q(s):
        return pltpu.make_async_copy(q_stage.at[s * TILES + spot], q_near.at[s, me], own_sem.at[1, s])

    def place_of(group):
        return lax.rem(group, WT) * HALF + group // WT

    def send_kv(s, tile_at):
        for d in range(1, TILES):
            group = peer(d)
            send_kv_tile(s, place_of(group), tile_at, group)
        own_kv(s, tile_at).start()

    def send_q(s):
        for d in range(1, TILES):
            group = peer(d)
            send_q_tile(s, place_of(group), group)
        own_q(s).start()

    def send_half(s):
        for i in range(1, HALF):
            place = lax.rem(chip + i, HALF)
            send_kv_tile(s, place, near_tile, place * WT)
        for i in range(1, HALF):
            place = lax.rem(chip + i, HALF)
            send_q_tile(s, place, place * WT)

        @pl.when(column == 0)
        def _():
            own_kv(s, near_tile).start()
            own_q(s).start()

        @pl.when(column == 1)
        def _():
            send_kv_tile(s, chip, near_tile, sibling)
            send_q_tile(s, chip, sibling)

    def halo_copies(s):
        return [
            remote(
                kv_wide.at[s, 1], kv_wide.at[s, 2 * side],
                halo_send.at[s, side], halo_recv.at[s, side], frame, me,
            )
            for side, frame in enumerate((later, earlier))
        ]

    row_parts = row_heads // HALF

    def part_of(f, part):
        return kv_row.at[f, column, pl.ds(part * HALF, HALF)]

    def staged_part(part):
        return kv_stage.at[pl.ds(row_base + part * HALF, HALF)]

    def row_halo(part):
        return [
            remote(
                staged_part(part), part_of(2 * side, part),
                row_send.at[part, side], row_recv.at[part, side], frame, me,
            )
            for side, frame in enumerate((later, earlier))
        ]

    def to_sibling(f, part):
        return remote(
            staged_part(part) if f == 1 else part_of(f, part), part_of(f, part),
            side_send.at[f, part], side_recv.at[f, part], seq, sibling,
        )

    def own_row():
        rows = pl.ds(row_base, row_heads)
        return [
            pltpu.make_async_copy(kv_stage.at[rows], kv_row.at[1, column], row_sem.at[0]),
            pltpu.make_async_copy(q_stage.at[rows], q_row, row_sem.at[1]),
        ]

    def start_wide_kv(s, carry):
        send_kv(s, wide_tile)
        return carry

    def start_q(s, carry):
        send_q(s)
        return carry

    def start_near(s, carry):
        send_kv(s, near_tile)
        send_q(s)
        return carry

    def forward(s, carry):
        bytes_of(kv_wide.at[s, 1, pl.ds(0, TILES - 1)], kv_recv.at[s]).wait()
        own_kv(s, wide_tile).wait()
        for copy in halo_copies(s):
            copy.start()
        return carry

    send_kv(0, wide_tile)
    if row_heads:
        for copy in row_halo(0):
            copy.start()
    lax.fori_loop(1, wide, start_wide_kv, 0)
    for part in range(row_parts):
        to_sibling(1, part).start()
    if row_heads:
        for copy in own_row():
            copy.start()
    lax.fori_loop(0, wide, start_q, 0)
    if full > wide:
        lax.fori_loop(wide, full, start_near, 0)
    if half:
        send_half(full)
    lax.fori_loop(0, 2, forward, 0)
    if row_heads:
        for side, copy in enumerate(row_halo(0)):
            copy.wait_recv()
            to_sibling(2 * side, 0).start()
    lax.fori_loop(2, wide, forward, 0)
    if row_heads:
        for copy in row_halo(1):
            copy.start()

    def row_pairs(part, frames):
        def heads(i, carry):
            for j in range(2):
                head = part * HALF + i * 2 + j
                o_row[head] = attend_row(q_row[head], kv_row, frames, head, table)
            return carry

        lax.fori_loop(0, HALF // 2, heads, 0)

    def row_part(part, frames):
        for f in frames:
            to_sibling(f, part).wait_recv()
        row_pairs(part, frames)

    table_load.wait()
    if row_heads:
        for copy in own_row():
            copy.wait()
        row_part(0, (0, 1, 2))
    if row_parts > 2:
        row_part(2, (1,))

    def attend_slot(s, kv_ref, first_frame):
        bytes_of(q_near.at[s, pl.ds(0, TILES - 1)], q_recv.at[s]).wait()
        own_q(s).wait()

        def write(t, tile):
            o_stage[s, t] = tile

        attend(q_near.at[s], kv_ref, (scores_a, scores_b), write, table, s, first_frame)
        position = s * TILES + spot
        for d in range(1, TILES):
            group = peer(d)
            remote(
                o_stage.at[s, group], out.at[position], o_send.at[s], o_recv.at[s], seq, group
            ).start()
        pltpu.make_async_copy(o_stage.at[s, me], out.at[position], own_sem.at[2, s]).start()

    def wide_slot(s, carry):
        for copy in halo_copies(s):
            copy.wait_recv()
        attend_slot(s, kv_wide.at[s], 0)
        return carry

    def near_slot(s, carry):
        bytes_of(kv_near.at[s - wide, 0, pl.ds(0, TILES - 1)], kv_recv.at[s]).wait()
        own_kv(s, near_tile).wait()
        attend_slot(s, kv_near.at[s - wide], 1)
        return carry

    near = slots - wide
    first = max(wide - near, 0)

    def pair(j, carry):
        if half:
            @pl.when((wide + j < full) | (column == 0))
            def _():
                near_slot(wide + j, 0)
        else:
            near_slot(wide + j, 0)
        wide_slot(first + j, 0)
        return carry

    if first:
        lax.fori_loop(0, first, wide_slot, 0)
    if near:
        lax.fori_loop(0, near, pair, 0)

    if row_heads:
        for side, copy in enumerate(row_halo(1)):
            copy.wait_recv()
            to_sibling(2 * side, 1).start()
        row_part(1, (0, 1, 2))
        pltpu.make_async_copy(o_row, out.at[pl.ds(row_base, row_heads)], row_sem.at[2]).start()

    def own_out(s):
        return pltpu.make_async_copy(o_stage.at[s, me], out.at[s * TILES + spot], own_sem.at[2, s])

    def sent_inputs(s, count):
        bytes_of(kv_stage.at[pl.ds(s * TILES, count)], kv_send.at[s]).wait()
        bytes_of(q_stage.at[pl.ds(s * TILES, count)], q_send.at[s]).wait()

    def got_outputs(s, count):
        bytes_of(out.at[pl.ds(s * TILES, count)], o_recv.at[s]).wait()

    def sent_outputs(s):
        own_out(s).wait()
        bytes_of(o_stage.at[s, pl.ds(0, TILES - 1)], o_send.at[s]).wait()

    def finish(s, carry):
        sent_inputs(s, TILES - 1)
        sent_outputs(s)
        got_outputs(s, TILES - 1)
        return carry

    def finish_halo(s, carry):
        for copy in halo_copies(s):
            copy.wait_send()
        return carry

    lax.fori_loop(0, wide, finish_halo, 0)
    for part in range(min(row_parts, 2)):
        for copy in row_halo(part):
            copy.wait_send()
    for part in range(row_parts):
        for f in (0, 1, 2) if part < 2 else (1,):
            to_sibling(f, part).wait_send()
    if row_heads:
        pltpu.make_async_copy(o_row, out.at[pl.ds(row_base, row_heads)], row_sem.at[2]).wait()
    if half:
        @pl.when(column == 0)
        def _():
            sent_inputs(full, HALF - 1)
            sent_outputs(full)
            got_outputs(full, HALF - 1)

        @pl.when(column == 1)
        def _():
            sent_inputs(full, HALF)
            got_outputs(full, HALF)
    lax.fori_loop(0, full, finish, 0)


def exchange(halves, wide, collective_id, frame_total, table, kv_stage, q_stage):
    slots = (halves + 1) // 2
    near = max(slots - wide, 1)
    row_heads = max(H - halves * HALF, 1)
    hbm = pl.BlockSpec(memory_space=pl.ANY)
    bf16 = jnp.bfloat16
    tile = (TILE, HD)
    dma = pltpu.SemaphoreType.DMA
    scores = pltpu.VMEM((FRAMES * TILES * TILE, WT * TILE), jnp.float32)
    return pl.pallas_call(
        functools.partial(exchange_kernel, halves, wide, frame_total),
        out_shape=jax.ShapeDtypeStruct((H,) + tile, bf16),
        in_specs=[hbm] * 3,
        out_specs=hbm,
        scratch_shapes=[
            pltpu.SMEM((TABLE,), jnp.float32),
            pltpu.VMEM((wide, FRAMES, TILES, 2) + tile, bf16),
            pltpu.VMEM((near, 1, TILES, 2) + tile, bf16),
            pltpu.VMEM((FRAMES, WT, row_heads, 2) + tile, bf16),
            pltpu.VMEM((slots, TILES) + tile, bf16),
            pltpu.VMEM((row_heads,) + tile, bf16),
            pltpu.VMEM((slots, TILES) + tile, bf16),
            pltpu.VMEM((row_heads,) + tile, bf16),
            scores, scores,
            dma((1,)),
            dma((slots,)), dma((slots,)), dma((slots,)), dma((slots,)),
            dma((wide, 2)), dma((wide, 2)),
            dma((slots,)), dma((slots,)), dma((3, slots)),
            dma((2, 2)), dma((2, 2)),
            dma((FRAMES, FRAMES)), dma((FRAMES, FRAMES)),
            dma((3,)),
        ],
        compiler_params=pltpu.CompilerParams(
            collective_id=collective_id, has_side_effects=True, vmem_limit_bytes=60 << 20
        ),
        name=f"exchange_{halves}_{wide}",
    )(table, kv_stage, q_stage)


def power(exponent):
    return jnp.where(exponent > 0, 2.0, jnp.where(exponent < 0, 0.5, 1.0)).astype(jnp.float32)


def prepare_kernel(
    frame_total,
    extents, q_exp, k_exp, v_exp, q_data, k_data, v_data,
    table, place, plan, kv_out, q_out,
    order, q_in, k_in, v_in, kv_stage, q_stage, in_sem, out_sem,
):
    loads = [
        pltpu.make_async_copy(src, dst, in_sem.at[i])
        for i, (src, dst) in enumerate(((k_data, k_in), (v_data, v_in), (q_data, q_in)))
    ]
    for load in loads:
        load.start()

    zero = jnp.int32(0)
    one = jnp.int32(1)

    def flag(condition):
        return jnp.where(condition, one, zero)

    reach = [flag(extents[0, h] >= 1) for h in range(H)]
    flat = [flag(extents[1, h] <= 0) for h in range(H)]
    reaching = sum(reach, zero)
    flat_reaching = sum((r * f for r, f in zip(reach, flat)), zero)
    row_reaching = jnp.minimum(flat_reaching, ROW_REACH)
    row_most = row_reaching + sum(flat, zero) - flat_reaching
    fits = flag(reaching - row_reaching <= PLANS[0][1] * TILES)
    twelve = fits * flag(row_most >= ROW_HEADS)
    eight = fits * flag(row_most >= TILES) * (1 - twelve)
    row_count = twelve * ROW_HEADS + eight * TILES
    row_reaching = flag(row_count > 0) * row_reaching
    row_base = H - row_count
    plan[0] = jnp.where(twelve > 0, 0, jnp.where(eight > 0, 1, 2))
    next_reach, next_rest = zero, reaching - row_reaching
    next_row_reach, next_row_rest = zero, row_reaching
    for h in range(H):
        row_index = jnp.where(reach[h] > 0, next_row_reach, next_row_rest)
        row_end = jnp.where(reach[h] > 0, row_reaching, row_count)
        in_row = flat[h] * flag(row_index < row_end)
        outside = 1 - in_row
        other = jnp.where(reach[h] > 0, next_reach, next_rest)
        position = jnp.where(in_row > 0, row_base + row_index, other)
        next_row_reach += in_row * reach[h]
        next_row_rest += in_row * (1 - reach[h])
        next_reach += outside * reach[h]
        next_rest += outside * (1 - reach[h])
        order[position] = h
        place[h] = position
    me = lax.axis_index("head")
    seq = lax.axis_index("seq")
    column = lax.rem(me, WT)
    spot = column * HALF + me // WT

    def within(condition):
        return jnp.where(condition, 0.0, NEG).astype(jnp.float32)

    def beside(head, f):
        inside = (seq + f - 1 >= 0) & (seq + f - 1 < frame_total)
        return within((extents[0, head] >= abs(f - 1)) & inside)

    for s in range(SLOTS):
        head = order[s * TILES + spot]
        entry = s * ENTRIES
        for r in range(HT):
            for t in range(HT):
                table[entry + r * HT + t] = within(extents[1, head] >= abs(r - t))
        for c in range(WT):
            table[entry + HT * HT + c] = within(extents[2, head] >= c)
        for f in range(FRAMES):
            table[entry + HT * HT + WT + f] = beside(head, f)
    for i in range(ROW_HEADS):
        head = order[jnp.minimum(row_base + i, H - 1)]
        entry = ROW_TABLE + i * ROW_ENTRIES
        for c in range(WT):
            table[entry + c] = within(extents[2, head] >= jnp.abs(column - c))
        for f in range(FRAMES):
            table[entry + WT + f] = beside(head, f)


    def scaled(ref, exps, head):
        columns = pl.ds(pl.multiple_of(head * HD, HD), HD)
        return (ref[:, columns].astype(jnp.float32) * power(exps[0, head])).astype(jnp.bfloat16)

    def slot_of(s):
        return pl.ds(s * TILES, TILES)

    def kv_copy(s, which):
        rows = slot_of(s)
        return pltpu.make_async_copy(
            kv_stage.at[rows, which], kv_out.at[rows, which], out_sem.at[which, s]
        )

    def q_copy(s):
        return pltpu.make_async_copy(q_stage.at[slot_of(s)], q_out.at[slot_of(s)], out_sem.at[2, s])

    def stage_keys(s, carry):
        for p in range(TILES):
            kv_stage[s * TILES + p, 0] = scaled(k_in, k_exp, order[s * TILES + p])
        kv_copy(s, 0).start()
        return carry

    def stage_values(s, carry):
        for p in range(TILES):
            kv_stage[s * TILES + p, 1] = scaled(v_in, v_exp, order[s * TILES + p]).T
        kv_copy(s, 1).start()
        return carry

    def stage_queries(s, carry):
        for p in range(TILES):
            q_stage[s * TILES + p] = scaled(q_in, q_exp, order[s * TILES + p])
        q_copy(s).start()
        return carry

    for load, stage in zip(loads, (stage_keys, stage_values, stage_queries)):
        load.wait()
        lax.fori_loop(0, SLOTS, stage, 0)
    for s in range(SLOTS):
        kv_copy(s, 0).wait()
        kv_copy(s, 1).wait()
        q_copy(s).wait()


def prepare(frame_total, extents, q_exp, k_exp, v_exp, q_data, k_data, v_data):
    smem = pl.BlockSpec(memory_space=pltpu.SMEM)
    hbm = pl.BlockSpec(memory_space=pl.ANY)
    bf16 = jnp.bfloat16
    kv = (H, 2, TILE, HD)
    q = (H, TILE, HD)
    whole = pltpu.VMEM((TILE, H * HD), bf16)
    return pl.pallas_call(
        functools.partial(prepare_kernel, frame_total),
        out_shape=(
            jax.ShapeDtypeStruct((TABLE,), jnp.float32),
            jax.ShapeDtypeStruct((H,), jnp.int32),
            jax.ShapeDtypeStruct((1,), jnp.int32),
            jax.ShapeDtypeStruct(kv, bf16),
            jax.ShapeDtypeStruct(q, bf16),
        ),
        in_specs=[smem] * 4 + [hbm] * 3,
        out_specs=(smem, smem, smem, hbm, hbm),
        scratch_shapes=[
            pltpu.SMEM((H,), jnp.int32),
            whole, whole, whole,
            pltpu.VMEM(kv, bf16),
            pltpu.VMEM(q, bf16),
            pltpu.SemaphoreType.DMA((3,)),
            pltpu.SemaphoreType.DMA((3, SLOTS)),
        ],
        compiler_params=pltpu.CompilerParams(vmem_limit_bytes=60 << 20),
        name="prepare",
    )(extents, q_exp, k_exp, v_exp, q_data, k_data, v_data)


def restore_kernel(place, tiles, out, held, in_sem, out_sem):
    parts = out_sem.shape[0]
    heads = H // parts

    def block(ref, i):
        return ref.at[:, pl.ds(i * heads * HD, heads * HD)]

    for h in range(H):
        columns = held.at[:, pl.ds(h * HD, HD)]
        pltpu.make_async_copy(tiles.at[place[h]], columns, in_sem.at[h // heads]).start()
    for i in range(parts):
        bytes_of(block(held, i), in_sem.at[i]).wait()
        pltpu.make_async_copy(block(held, i), block(out, i), out_sem.at[i]).start()
    for i in range(parts):
        pltpu.make_async_copy(block(held, i), block(out, i), out_sem.at[i]).wait()


def restore(place, tiles):
    hbm = pl.BlockSpec(memory_space=pl.ANY)
    return pl.pallas_call(
        restore_kernel,
        out_shape=jax.ShapeDtypeStruct((TILE, H * HD), jnp.bfloat16),
        in_specs=[pl.BlockSpec(memory_space=pltpu.SMEM), hbm],
        out_specs=hbm,
        scratch_shapes=[
            pltpu.VMEM((TILE, H * HD), jnp.bfloat16),
            pltpu.SemaphoreType.DMA((4,)),
            pltpu.SemaphoreType.DMA((4,)),
        ],
        compiler_params=pltpu.CompilerParams(vmem_limit_bytes=60 << 20),
        name="restore",
    )(place, tiles)


def on_device(frame_total, q_data, k_data, v_data, q_exp, k_exp, v_exp, extents):
    table, place, plan, kv_stage, q_stage = prepare(
        frame_total, extents.T, q_exp, k_exp, v_exp, q_data, k_data, v_data
    )
    branches = [
        functools.partial(exchange, halves, wide, i, frame_total)
        for i, (halves, wide) in enumerate(PLANS)
    ]
    tiles = lax.switch(plan[0], branches, table, kv_stage, q_stage)
    return restore(place, tiles)


def solution(mesh):
    rows = P(("seq", "head"), None)
    return jax.shard_map(
        functools.partial(on_device, mesh.shape["seq"]),
        mesh=mesh,
        in_specs=(rows,) * 6 + (P(),),
        out_specs=rows,
        check_vma=False,
    )
```

```python
import functools
import math

import jax
import jax.numpy as jnp
from jax import lax
from jax.experimental import pallas as pl
from jax.experimental.pallas import tpu as pltpu
from jax.sharding import PartitionSpec as P

H = 48
HD = 128
TILE = 128
HT = 4
WT = 2
TILES = HT * WT
HALF = TILES // 2
FRAMES = 3
NEG = -1e30
LOG2_SCALE = math.log2(math.e) / math.sqrt(HD)
MESH = pl.DeviceIdType.MESH

PLANS = ((9, 3), (10, 3), (11, 3), (12, 6))
ROW_HEADS = 12
ROW_REACH = 8

SLOTS = H // TILES
ENTRIES = HT * HT + WT + FRAMES
ROW_TABLE = SLOTS * ENTRIES
ROW_ENTRIES = WT + FRAMES
TABLE = ROW_TABLE + ROW_HEADS * ROW_ENTRIES


def bytes_of(ref, sem):
    return pltpu.make_async_copy(ref, ref, sem)


def block_max(s):
    return jnp.max(s.reshape(s.shape[0] // 8, 8, s.shape[1]), axis=0)


def attend(q_ref, kv_ref, score_refs, write, table, slot, first_frame):
    frames = kv_ref.shape[0]
    entry = slot * ENTRIES

    def biases(row):
        rows = [table[entry + row * HT + r] for r in range(HT)]
        columns = [table[entry + HT * HT + c] for c in range(WT)]
        beside = [table[entry + HT * HT + WT + first_frame + f] for f in range(frames)]
        return lambda f, t, u: rows[t // WT] + columns[abs(t % WT - u)] + beside[f]

    def score(row, s_ref):
        bias = biases(row)
        queries = q_ref[pl.ds(row * WT, WT)].reshape(WT * TILE, HD)
        peak = [None] * WT
        for f in range(frames):
            for t in range(0, TILES, WT):
                keys = kv_ref[f, t : t + WT, 0].reshape(WT * TILE, HD)
                s = lax.dot_general(
                    keys, queries, (((1,), (1,)), ((), ())), preferred_element_type=jnp.float32
                )
                base = (f * TILES + t) * TILE
                s_ref[base : base + WT * TILE, :] = s
                for j in range(WT):
                    for u in range(WT):
                        block = s[j * TILE : (j + 1) * TILE, u * TILE : (u + 1) * TILE]
                        top = block_max(block) + bias(f, t + j, u)
                        peak[u] = top if peak[u] is None else jnp.maximum(peak[u], top)
        return [jnp.max(p, axis=0, keepdims=True) * LOG2_SCALE for p in peak]

    def combine(row, s_ref, peak):
        bias = biases(row)
        ones = jnp.ones((16, WT * TILE), jnp.bfloat16)
        total = None
        for f in range(frames):
            for t in range(0, TILES, WT):
                base = (f * TILES + t) * TILE
                columns = []
                for u in range(WT):
                    parts = []
                    for j in range(WT):
                        s = s_ref[base + j * TILE : base + (j + 1) * TILE, u * TILE : (u + 1) * TILE]
                        shift = bias(f, t + j, u) - peak[u]
                        parts.append(jnp.exp2(s * LOG2_SCALE + shift).astype(jnp.bfloat16))
                    columns.append(jnp.concatenate(parts, axis=0))
                weights = jnp.concatenate(columns, axis=1)
                values = jnp.concatenate([kv_ref[f, t + j, 1] for j in range(WT)], axis=1)
                values = jnp.concatenate([values, ones], axis=0)
                part = jnp.dot(values, weights, preferred_element_type=jnp.float32)
                total = part if total is None else total + part
        out = total[:HD] * (1.0 / total[HD : HD + 1])
        for u in range(WT):
            write(row * WT + u, out[:, u * TILE : (u + 1) * TILE].T.astype(jnp.bfloat16))

    def rows(i, carry):
        at = [i * 2 + j for j in range(2)]
        peaks = [score(r, s_ref) for r, s_ref in zip(at, score_refs)]
        for r, s_ref, peak in zip(at, score_refs, peaks):
            combine(r, s_ref, peak)
        return carry

    lax.fori_loop(0, HT // 2, rows, 0)


def attend_row(queries, kv_ref, frames, head, table):
    entry = ROW_TABLE + head * ROW_ENTRIES
    columns = [table[entry + c] for c in range(WT)]
    blocks = [(f, c, columns[c] + table[entry + WT + f]) for f in frames for c in range(WT)]
    scores = []
    peak = None
    for f, c, bias in blocks:
        s = lax.dot_general(
            kv_ref[f, c, head, 0], queries, (((1,), (1,)), ((), ())), preferred_element_type=jnp.float32
        )
        scores.append(s)
        top = block_max(s) + bias
        peak = top if peak is None else jnp.maximum(peak, top)
    peak = jnp.max(peak, axis=0, keepdims=True) * LOG2_SCALE
    weights = jnp.concatenate(
        [jnp.exp2(s * LOG2_SCALE + (bias - peak)) for s, (_, _, bias) in zip(scores, blocks)], axis=0
    ).astype(jnp.bfloat16)
    values = jnp.concatenate([kv_ref[f, c, head, 1] for f, c, _ in blocks], axis=1)
    values = jnp.concatenate([values, jnp.ones((16, values.shape[1]), jnp.bfloat16)], axis=0)
    total = jnp.dot(values, weights, preferred_element_type=jnp.float32)
    return (total[:HD] * (1.0 / total[HD : HD + 1])).T.astype(jnp.bfloat16)


def exchange_kernel(
    halves, wide, frame_total,
    table_hbm, kv_stage, q_stage,
    out,
    table, kv_wide, kv_near, kv_row, q_near, q_row, o_stage, o_row, scores_a, scores_b,
    table_sem, kv_send, kv_recv, q_send, q_recv, halo_send, halo_recv, o_send, o_recv, own_sem,
    row_send, row_recv, side_send, side_recv, row_sem,
):
    full, half = halves // 2, halves % 2
    slots = full + half
    row_base = halves * HALF
    row_heads = H - row_base
    me = lax.axis_index("head")
    seq = lax.axis_index("seq")
    later = lax.rem(seq + 1, frame_total)
    earlier = lax.rem(seq + frame_total - 1, frame_total)
    column = lax.rem(me, WT)
    chip = me // WT
    sibling = me + 1 - 2 * column
    spot = column * HALF + chip

    table_load = pltpu.make_async_copy(table_hbm, table, table_sem.at[0])
    table_load.start()

    def peer(d):
        return lax.rem(me + d, TILES)

    barrier = pltpu.get_barrier_semaphore()
    for d in range(1, TILES):
        pl.semaphore_signal(barrier, inc=1, device_id=(seq, peer(d)), device_id_type=MESH)
    for frame in (later, earlier):
        pl.semaphore_signal(barrier, inc=1, device_id=(frame, me), device_id_type=MESH)
    pl.semaphore_wait(barrier, TILES - 1 + 2)

    def remote(src, dst, send, recv, frame, group):
        return pltpu.make_async_remote_copy(
            src_ref=src, dst_ref=dst, send_sem=send, recv_sem=recv,
            device_id=(frame, group), device_id_type=MESH,
        )

    def wide_tile(s, t):
        return kv_wide.at[s, 1, t]

    def near_tile(s, t):
        return kv_near.at[s - wide, 0, t]

    def send_kv_tile(s, place, tile_at, group):
        src = kv_stage.at[s * TILES + place]
        remote(src, tile_at(s, me), kv_send.at[s], kv_recv.at[s], seq, group).start()

    def send_q_tile(s, place, group):
        src = q_stage.at[s * TILES + place]
        remote(src, q_near.at[s, me], q_send.at[s], q_recv.at[s], seq, group).start()

    def own_kv(s, tile_at):
        return pltpu.make_async_copy(kv_stage.at[s * TILES + spot], tile_at(s, me), own_sem.at[0, s])

    def own_q(s):
        return pltpu.make_async_copy(q_stage.at[s * TILES + spot], q_near.at[s, me], own_sem.at[1, s])

    def place_of(group):
        return lax.rem(group, WT) * HALF + group // WT

    def send_kv(s, tile_at):
        for d in range(1, TILES):
            group = peer(d)
            send_kv_tile(s, place_of(group), tile_at, group)
        own_kv(s, tile_at).start()

    def send_q(s):
        for d in range(1, TILES):
            group = peer(d)
            send_q_tile(s, place_of(group), group)
        own_q(s).start()

    def send_half(s):
        for i in range(1, HALF):
            place = lax.rem(chip + i, HALF)
            send_kv_tile(s, place, near_tile, place * WT)
        for i in range(1, HALF):
            place = lax.rem(chip + i, HALF)
            send_q_tile(s, place, place * WT)

        @pl.when(column == 0)
        def _():
            own_kv(s, near_tile).start()
            own_q(s).start()

        @pl.when(column == 1)
        def _():
            send_kv_tile(s, chip, near_tile, sibling)
            send_q_tile(s, chip, sibling)

    def halo_copies(s):
        return [
            remote(
                kv_wide.at[s, 1], kv_wide.at[s, 2 * side],
                halo_send.at[s, side], halo_recv.at[s, side], frame, me,
            )
            for side, frame in enumerate((later, earlier))
        ]

    row_parts = row_heads // HALF
    reach_parts = min(row_parts, 2)

    def part_of(f, part):
        return kv_row.at[f, column, pl.ds(part * HALF, HALF)]

    def staged_part(part):
        return kv_stage.at[pl.ds(row_base + part * HALF, HALF)]

    def row_halo(part):
        return [
            remote(
                staged_part(part), part_of(2 * side, part),
                row_send.at[part, side], row_recv.at[part, side], frame, me,
            )
            for side, frame in enumerate((later, earlier))
        ]

    def to_sibling(f, part):
        return remote(
            staged_part(part) if f == 1 else part_of(f, part), part_of(f, part),
            side_send.at[f, part], side_recv.at[f, part], seq, sibling,
        )

    def own_row():
        rows = pl.ds(row_base, row_heads)
        return [
            pltpu.make_async_copy(kv_stage.at[rows], kv_row.at[1, column], row_sem.at[0]),
            pltpu.make_async_copy(q_stage.at[rows], q_row, row_sem.at[1]),
        ]

    def start_wide_kv(s, carry):
        send_kv(s, wide_tile)
        return carry

    def start_q(s, carry):
        send_q(s)
        return carry

    def start_near(s, carry):
        send_kv(s, near_tile)
        send_q(s)
        return carry

    def forward(s, carry):
        bytes_of(kv_wide.at[s, 1, pl.ds(0, TILES - 1)], kv_recv.at[s]).wait()
        own_kv(s, wide_tile).wait()
        for copy in halo_copies(s):
            copy.start()
        return carry

    send_kv(0, wide_tile)
    if row_heads:
        for copy in row_halo(0):
            copy.start()
    lax.fori_loop(1, wide, start_wide_kv, 0)
    for part in range(row_parts):
        to_sibling(1, part).start()
    if row_heads:
        for copy in own_row():
            copy.start()
    lax.fori_loop(0, wide, start_q, 0)
    if full > wide:
        lax.fori_loop(wide, full, start_near, 0)
    if half:
        send_half(full)
    lax.fori_loop(0, 2, forward, 0)
    if row_heads:
        for side, copy in enumerate(row_halo(0)):
            copy.wait_recv()
            to_sibling(2 * side, 0).start()
    lax.fori_loop(2, wide, forward, 0)
    if reach_parts > 1:
        for copy in row_halo(1):
            copy.start()

    def row_pairs(part, frames):
        def heads(i, carry):
            for j in range(2):
                head = part * HALF + i * 2 + j
                o_row[head] = attend_row(q_row[head], kv_row, frames, head, table)
            return carry

        lax.fori_loop(0, HALF // 2, heads, 0)

    def row_part(part, frames):
        for f in frames:
            to_sibling(f, part).wait_recv()
        row_pairs(part, frames)

    table_load.wait()
    if row_heads:
        for copy in own_row():
            copy.wait()
        row_part(0, (0, 1, 2))
    for part in range(2, row_parts):
        row_part(part, (1,))

    def attend_slot(s, kv_ref, first_frame):
        bytes_of(q_near.at[s, pl.ds(0, TILES - 1)], q_recv.at[s]).wait()
        own_q(s).wait()

        def write(t, tile):
            o_stage[s, t] = tile

        attend(q_near.at[s], kv_ref, (scores_a, scores_b), write, table, s, first_frame)
        position = s * TILES + spot
        for d in range(1, TILES):
            group = peer(d)
            remote(
                o_stage.at[s, group], out.at[position], o_send.at[s], o_recv.at[s], seq, group
            ).start()
        pltpu.make_async_copy(o_stage.at[s, me], out.at[position], own_sem.at[2, s]).start()

    def wide_slot(s, carry):
        for copy in halo_copies(s):
            copy.wait_recv()
        attend_slot(s, kv_wide.at[s], 0)
        return carry

    def near_slot(s, carry):
        bytes_of(kv_near.at[s - wide, 0, pl.ds(0, TILES - 1)], kv_recv.at[s]).wait()
        own_kv(s, near_tile).wait()
        attend_slot(s, kv_near.at[s - wide], 1)
        return carry

    near = slots - wide
    first = max(wide - near, 0)

    def pair(j, carry):
        if half:
            @pl.when((wide + j < full) | (column == 0))
            def _():
                near_slot(wide + j, 0)
        else:
            near_slot(wide + j, 0)
        wide_slot(first + j, 0)
        return carry

    if first:
        lax.fori_loop(0, first, wide_slot, 0)
    if near:
        lax.fori_loop(0, near, pair, 0)

    if reach_parts > 1:
        for side, copy in enumerate(row_halo(1)):
            copy.wait_recv()
            to_sibling(2 * side, 1).start()
        row_part(1, (0, 1, 2))
    if row_heads:
        pltpu.make_async_copy(o_row, out.at[pl.ds(row_base, row_heads)], row_sem.at[2]).start()

    def own_out(s):
        return pltpu.make_async_copy(o_stage.at[s, me], out.at[s * TILES + spot], own_sem.at[2, s])

    def sent_inputs(s, count):
        bytes_of(kv_stage.at[pl.ds(s * TILES, count)], kv_send.at[s]).wait()
        bytes_of(q_stage.at[pl.ds(s * TILES, count)], q_send.at[s]).wait()

    def got_outputs(s, count):
        bytes_of(out.at[pl.ds(s * TILES, count)], o_recv.at[s]).wait()

    def sent_outputs(s):
        own_out(s).wait()
        bytes_of(o_stage.at[s, pl.ds(0, TILES - 1)], o_send.at[s]).wait()

    def finish(s, carry):
        sent_inputs(s, TILES - 1)
        sent_outputs(s)
        got_outputs(s, TILES - 1)
        return carry

    def finish_halo(s, carry):
        for copy in halo_copies(s):
            copy.wait_send()
        return carry

    lax.fori_loop(0, wide, finish_halo, 0)
    for part in range(reach_parts):
        for copy in row_halo(part):
            copy.wait_send()
    for part in range(row_parts):
        for f in (0, 1, 2) if part < 2 else (1,):
            to_sibling(f, part).wait_send()
    if row_heads:
        pltpu.make_async_copy(o_row, out.at[pl.ds(row_base, row_heads)], row_sem.at[2]).wait()
    if half:
        @pl.when(column == 0)
        def _():
            sent_inputs(full, HALF - 1)
            sent_outputs(full)
            got_outputs(full, HALF - 1)

        @pl.when(column == 1)
        def _():
            sent_inputs(full, HALF)
            got_outputs(full, HALF)
    lax.fori_loop(0, full, finish, 0)


def exchange(halves, wide, collective_id, frame_total, table, kv_stage, q_stage):
    slots = (halves + 1) // 2
    near = max(slots - wide, 1)
    row_heads = max(H - halves * HALF, 1)
    hbm = pl.BlockSpec(memory_space=pl.ANY)
    vmem = pl.BlockSpec(memory_space=pltpu.VMEM)
    bf16 = jnp.bfloat16
    tile = (TILE, HD)
    dma = pltpu.SemaphoreType.DMA
    scores = pltpu.VMEM((FRAMES * TILES * TILE, WT * TILE), jnp.float32)
    return pl.pallas_call(
        functools.partial(exchange_kernel, halves, wide, frame_total),
        out_shape=pltpu.VMEM((H,) + tile, bf16),
        in_specs=[hbm, vmem, vmem],
        out_specs=vmem,
        scratch_shapes=[
            pltpu.SMEM((TABLE,), jnp.float32),
            pltpu.VMEM((wide, FRAMES, TILES, 2) + tile, bf16),
            pltpu.VMEM((near, 1, TILES, 2) + tile, bf16),
            pltpu.VMEM((FRAMES, WT, row_heads, 2) + tile, bf16),
            pltpu.VMEM((slots, TILES) + tile, bf16),
            pltpu.VMEM((row_heads,) + tile, bf16),
            pltpu.VMEM((slots, TILES) + tile, bf16),
            pltpu.VMEM((row_heads,) + tile, bf16),
            scores, scores,
            dma((1,)),
            dma((slots,)), dma((slots,)), dma((slots,)), dma((slots,)),
            dma((wide, 2)), dma((wide, 2)),
            dma((slots,)), dma((slots,)), dma((3, slots)),
            dma((2, 2)), dma((2, 2)),
            dma((FRAMES, ROW_HEADS // HALF)), dma((FRAMES, ROW_HEADS // HALF)),
            dma((3,)),
        ],
        compiler_params=pltpu.CompilerParams(
            collective_id=collective_id, has_side_effects=True, vmem_limit_bytes=40 << 20
        ),
        name=f"exchange_{halves}_{wide}",
    )(table, kv_stage, q_stage)


def power(exponent):
    return jnp.where(exponent > 0, 2.0, jnp.where(exponent < 0, 0.5, 1.0)).astype(jnp.float32)


def prepare_kernel(
    frame_total,
    extents_hbm, q_exp_hbm, k_exp_hbm, v_exp_hbm, q_data, k_data, v_data,
    table, place, plan, kv_stage, q_stage,
    extents, q_exp, k_exp, v_exp, order, q_in, k_in, v_in, in_sem, small_sem,
):
    loads = [
        pltpu.make_async_copy(src, dst, in_sem.at[i])
        for i, (src, dst) in enumerate(((k_data, k_in), (v_data, v_in), (q_data, q_in)))
    ]
    small = [
        pltpu.make_async_copy(src, dst, small_sem.at[i])
        for i, (src, dst) in enumerate(
            (
                (extents_hbm, extents),
                (k_exp_hbm, k_exp),
                (v_exp_hbm, v_exp),
                (q_exp_hbm, q_exp),
            )
        )
    ]
    for load in small + loads:
        load.start()
    for load in small:
        load.wait()

    zero = jnp.int32(0)
    one = jnp.int32(1)

    def flag(condition):
        return jnp.where(condition, one, zero)

    reach = [flag(extents[0, h] >= 1) for h in range(H)]
    flat = [flag(extents[1, h] <= 0) for h in range(H)]
    reaching = sum(reach, zero)
    flat_reaching = sum((r * f for r, f in zip(reach, flat)), zero)
    row_reaching = jnp.minimum(flat_reaching, ROW_REACH)
    row_most = row_reaching + sum(flat, zero) - flat_reaching
    row_count = zero
    for count in range(HALF, ROW_HEADS + 1, HALF):
        fits = reaching - jnp.minimum(row_reaching, count) <= PLANS[0][1] * TILES
        row_count = jnp.where(fits & (row_most >= count), count, row_count)
    row_reaching = jnp.minimum(row_reaching, row_count)
    row_base = H - row_count
    plan[0] = len(PLANS) - 1 - row_count // HALF
    next_reach, next_rest = zero, reaching - row_reaching
    next_row_reach, next_row_rest = zero, row_reaching
    for h in range(H):
        row_index = jnp.where(reach[h] > 0, next_row_reach, next_row_rest)
        row_end = jnp.where(reach[h] > 0, row_reaching, row_count)
        in_row = flat[h] * flag(row_index < row_end)
        outside = 1 - in_row
        other = jnp.where(reach[h] > 0, next_reach, next_rest)
        position = jnp.where(in_row > 0, row_base + row_index, other)
        next_row_reach += in_row * reach[h]
        next_row_rest += in_row * (1 - reach[h])
        next_reach += outside * reach[h]
        next_rest += outside * (1 - reach[h])
        order[position] = h
        place[h] = position
    me = lax.axis_index("head")
    seq = lax.axis_index("seq")
    column = lax.rem(me, WT)
    spot = column * HALF + me // WT

    def within(condition):
        return jnp.where(condition, 0.0, NEG).astype(jnp.float32)

    def beside(head, f):
        inside = (seq + f - 1 >= 0) & (seq + f - 1 < frame_total)
        return within((extents[0, head] >= abs(f - 1)) & inside)

    for s in range(SLOTS):
        head = order[s * TILES + spot]
        entry = s * ENTRIES
        for r in range(HT):
            for t in range(HT):
                table[entry + r * HT + t] = within(extents[1, head] >= abs(r - t))
        for c in range(WT):
            table[entry + HT * HT + c] = within(extents[2, head] >= c)
        for f in range(FRAMES):
            table[entry + HT * HT + WT + f] = beside(head, f)
    for i in range(ROW_HEADS):
        head = order[jnp.minimum(row_base + i, H - 1)]
        entry = ROW_TABLE + i * ROW_ENTRIES
        for c in range(WT):
            table[entry + c] = within(extents[2, head] >= jnp.abs(column - c))
        for f in range(FRAMES):
            table[entry + WT + f] = beside(head, f)


    def scaled(ref, exps, head):
        columns = pl.ds(pl.multiple_of(head * HD, HD), HD)
        return (ref[:, columns].astype(jnp.float32) * power(exps[0, head])).astype(jnp.bfloat16)

    def stage_keys(s, carry):
        for p in range(TILES):
            kv_stage[s * TILES + p, 0] = scaled(k_in, k_exp, order[s * TILES + p])
        return carry

    def stage_values(s, carry):
        for p in range(TILES):
            kv_stage[s * TILES + p, 1] = scaled(v_in, v_exp, order[s * TILES + p]).T
        return carry

    def stage_queries(s, carry):
        for p in range(TILES):
            q_stage[s * TILES + p] = scaled(q_in, q_exp, order[s * TILES + p])
        return carry

    for load, stage in zip(loads, (stage_keys, stage_values, stage_queries)):
        load.wait()
        lax.fori_loop(0, SLOTS, stage, 0)


def prepare(frame_total, extents, q_exp, k_exp, v_exp, q_data, k_data, v_data):
    smem = pl.BlockSpec(memory_space=pltpu.SMEM)
    bf16 = jnp.bfloat16
    kv = (H, 2, TILE, HD)
    q = (H, TILE, HD)
    vmem = pl.BlockSpec(memory_space=pltpu.VMEM)
    whole = pltpu.VMEM((TILE, H * HD), bf16)
    exponents = pltpu.SMEM((1, H), jnp.int32)
    return pl.pallas_call(
        functools.partial(prepare_kernel, frame_total),
        out_shape=(
            jax.ShapeDtypeStruct((TABLE,), jnp.float32),
            jax.ShapeDtypeStruct((H,), jnp.int32),
            jax.ShapeDtypeStruct((1,), jnp.int32),
            pltpu.VMEM(kv, bf16),
            pltpu.VMEM(q, bf16),
        ),
        in_specs=[pl.BlockSpec(memory_space=pltpu.HBM)] * 7,
        out_specs=(smem, smem, smem, vmem, vmem),
        scratch_shapes=[
            pltpu.SMEM((3, H), jnp.int32),
            exponents, exponents, exponents,
            pltpu.SMEM((H,), jnp.int32),
            whole, whole, whole,
            pltpu.SemaphoreType.DMA((3,)),
            pltpu.SemaphoreType.DMA((4,)),
        ],
        compiler_params=pltpu.CompilerParams(vmem_limit_bytes=58 << 20),
        name="prepare",
    )(extents, q_exp, k_exp, v_exp, q_data, k_data, v_data)


def restore_kernel(place, tiles, out, held, out_sem):
    parts = out_sem.shape[0]
    heads = H // parts

    def copy(i):
        columns = pl.ds(i * heads * HD, heads * HD)
        return pltpu.make_async_copy(held.at[:, columns], out.at[:, columns], out_sem.at[i])

    for i in range(parts):
        for h in range(i * heads, (i + 1) * heads):
            held[:, h * HD : (h + 1) * HD] = tiles[place[h]]
        copy(i).start()
    for i in range(parts):
        copy(i).wait()


def restore(place, tiles):
    return pl.pallas_call(
        restore_kernel,
        out_shape=jax.ShapeDtypeStruct((TILE, H * HD), jnp.bfloat16),
        in_specs=[
            pl.BlockSpec(memory_space=pltpu.SMEM),
            pl.BlockSpec(memory_space=pltpu.VMEM),
        ],
        out_specs=pl.BlockSpec(memory_space=pl.ANY),
        scratch_shapes=[
            pltpu.VMEM((TILE, H * HD), jnp.bfloat16),
            pltpu.SemaphoreType.DMA((8,)),
        ],
        compiler_params=pltpu.CompilerParams(vmem_limit_bytes=40 << 20),
        name="restore",
    )(place, tiles)


def on_device(frame_total, q_data, k_data, v_data, q_exp, k_exp, v_exp, extents):
    table, place, plan, kv_stage, q_stage = prepare(
        frame_total, extents.T, q_exp, k_exp, v_exp, q_data, k_data, v_data
    )
    branches = [
        functools.partial(exchange, halves, wide, i, frame_total)
        for i, (halves, wide) in enumerate(PLANS)
    ]
    tiles = lax.switch(plan[0], branches, table, kv_stage, q_stage)
    return restore(place, tiles)


def solution(mesh):
    rows = P(("seq", "head"), None)
    return jax.shard_map(
        functools.partial(on_device, mesh.shape["seq"]),
        mesh=mesh,
        in_specs=(rows,) * 6 + (P(),),
        out_specs=rows,
        check_vma=False,
    )
```

```python
import functools
import math

import jax
import jax.numpy as jnp
from jax import lax
from jax.experimental import pallas as pl
from jax.experimental.pallas import tpu as pltpu
from jax.sharding import PartitionSpec as P

H = 48
HD = 128
TILE = 128
HT = 4
WT = 2
TILES = HT * WT
HALF = TILES // 2
FRAMES = 3
NEG = -1e30
LOG2_SCALE = math.log2(math.e) / math.sqrt(HD)
MESH = pl.DeviceIdType.MESH

PLANS = ((9, 3), (10, 3), (11, 3), (12, 6))
ROW_HEADS = 12
ROW_REACH = 8

SLOTS = H // TILES
ENTRIES = HT * HT + WT + FRAMES
ROW_TABLE = SLOTS * ENTRIES
ROW_ENTRIES = WT + FRAMES
TABLE = ROW_TABLE + ROW_HEADS * ROW_ENTRIES


def bytes_of(ref, sem):
    return pltpu.make_async_copy(ref, ref, sem)


def block_max(s):
    return jnp.max(s.reshape(s.shape[0] // 8, 8, s.shape[1]), axis=0)


def attend(q_ref, kv_ref, score_refs, write, table, slot, first_frame):
    frames = kv_ref.shape[0]
    entry = slot * ENTRIES

    def biases(row):
        rows = [table[entry + row * HT + r] for r in range(HT)]
        columns = [table[entry + HT * HT + c] for c in range(WT)]
        beside = [table[entry + HT * HT + WT + first_frame + f] for f in range(frames)]
        return lambda f, t, u: rows[t // WT] + columns[abs(t % WT - u)] + beside[f]

    def score(row, s_ref):
        bias = biases(row)
        queries = q_ref[pl.ds(row * WT, WT)].reshape(WT * TILE, HD)
        peak = [None] * WT
        for f in range(frames):
            for t in range(0, TILES, WT):
                keys = kv_ref[f, t : t + WT, 0].reshape(WT * TILE, HD)
                s = lax.dot_general(
                    keys, queries, (((1,), (1,)), ((), ())), preferred_element_type=jnp.float32
                )
                base = (f * TILES + t) * TILE
                s_ref[base : base + WT * TILE, :] = s
                for j in range(WT):
                    for u in range(WT):
                        block = s[j * TILE : (j + 1) * TILE, u * TILE : (u + 1) * TILE]
                        top = block_max(block) + bias(f, t + j, u)
                        peak[u] = top if peak[u] is None else jnp.maximum(peak[u], top)
        return [jnp.max(p, axis=0, keepdims=True) * LOG2_SCALE for p in peak]

    def combine(row, s_ref, peak):
        bias = biases(row)
        ones = jnp.ones((16, WT * TILE), jnp.bfloat16)
        total = None
        for f in range(frames):
            for t in range(0, TILES, WT):
                base = (f * TILES + t) * TILE
                columns = []
                for u in range(WT):
                    parts = []
                    for j in range(WT):
                        s = s_ref[base + j * TILE : base + (j + 1) * TILE, u * TILE : (u + 1) * TILE]
                        shift = bias(f, t + j, u) - peak[u]
                        parts.append(jnp.exp2(s * LOG2_SCALE + shift).astype(jnp.bfloat16))
                    columns.append(jnp.concatenate(parts, axis=0))
                weights = jnp.concatenate(columns, axis=1)
                values = jnp.concatenate([kv_ref[f, t + j, 1] for j in range(WT)], axis=1)
                values = jnp.concatenate([values, ones], axis=0)
                part = jnp.dot(values, weights, preferred_element_type=jnp.float32)
                total = part if total is None else total + part
        out = total[:HD] * (1.0 / total[HD : HD + 1])
        for u in range(WT):
            write(row * WT + u, out[:, u * TILE : (u + 1) * TILE].T.astype(jnp.bfloat16))

    def rows(i, carry):
        at = [i * 2 + j for j in range(2)]
        peaks = [score(r, s_ref) for r, s_ref in zip(at, score_refs)]
        for r, s_ref, peak in zip(at, score_refs, peaks):
            combine(r, s_ref, peak)
        return carry

    lax.fori_loop(0, HT // 2, rows, 0)


def attend_row(queries, kv_ref, frames, head, table):
    entry = ROW_TABLE + head * ROW_ENTRIES
    columns = [table[entry + c] for c in range(WT)]
    blocks = [(f, c, columns[c] + table[entry + WT + f]) for f in frames for c in range(WT)]
    scores = []
    peak = None
    for f, c, bias in blocks:
        s = lax.dot_general(
            kv_ref[f, c, head, 0], queries, (((1,), (1,)), ((), ())), preferred_element_type=jnp.float32
        )
        scores.append(s)
        top = block_max(s) + bias
        peak = top if peak is None else jnp.maximum(peak, top)
    peak = jnp.max(peak, axis=0, keepdims=True) * LOG2_SCALE
    weights = jnp.concatenate(
        [jnp.exp2(s * LOG2_SCALE + (bias - peak)) for s, (_, _, bias) in zip(scores, blocks)], axis=0
    ).astype(jnp.bfloat16)
    values = jnp.concatenate([kv_ref[f, c, head, 1] for f, c, _ in blocks], axis=1)
    values = jnp.concatenate([values, jnp.ones((16, values.shape[1]), jnp.bfloat16)], axis=0)
    total = jnp.dot(values, weights, preferred_element_type=jnp.float32)
    return (total[:HD] * (1.0 / total[HD : HD + 1])).T.astype(jnp.bfloat16)


def exchange_kernel(
    halves, wide, frame_total,
    table, kv_stage, q_stage,
    out,
    kv_wide, kv_near, kv_row, q_near, q_row, o_stage, o_row, scores_a, scores_b,
    kv_send, kv_recv, q_send, q_recv, halo_send, halo_recv, o_send, o_recv, own_sem,
    row_send, row_recv, side_send, side_recv, row_sem,
):
    full, half = halves // 2, halves % 2
    slots = full + half
    row_base = halves * HALF
    row_heads = H - row_base
    me = lax.axis_index("head")
    seq = lax.axis_index("seq")
    later = lax.rem(seq + 1, frame_total)
    earlier = lax.rem(seq + frame_total - 1, frame_total)
    column = lax.rem(me, WT)
    chip = me // WT
    sibling = me + 1 - 2 * column
    spot = column * HALF + chip

    def peer(d):
        return lax.rem(me + d, TILES)

    barrier = pltpu.get_barrier_semaphore()
    for d in range(1, TILES):
        pl.semaphore_signal(barrier, inc=1, device_id=(seq, peer(d)), device_id_type=MESH)
    for frame in (later, earlier):
        pl.semaphore_signal(barrier, inc=1, device_id=(frame, me), device_id_type=MESH)
    pl.semaphore_wait(barrier, TILES - 1 + 2)

    def remote(src, dst, send, recv, frame, group):
        return pltpu.make_async_remote_copy(
            src_ref=src, dst_ref=dst, send_sem=send, recv_sem=recv,
            device_id=(frame, group), device_id_type=MESH,
        )

    def wide_tile(s, t):
        return kv_wide.at[s, 1, t]

    def near_tile(s, t):
        return kv_near.at[s - wide, 0, t]

    def send_kv_tile(s, place, tile_at, group):
        src = kv_stage.at[s * TILES + place]
        remote(src, tile_at(s, me), kv_send.at[s], kv_recv.at[s], seq, group).start()

    def send_q_tile(s, place, group):
        src = q_stage.at[s * TILES + place]
        remote(src, q_near.at[s, me], q_send.at[s], q_recv.at[s], seq, group).start()

    def own_kv(s, tile_at):
        return pltpu.make_async_copy(kv_stage.at[s * TILES + spot], tile_at(s, me), own_sem.at[0, s])

    def own_q(s):
        return pltpu.make_async_copy(q_stage.at[s * TILES + spot], q_near.at[s, me], own_sem.at[1, s])

    def place_of(group):
        return lax.rem(group, WT) * HALF + group // WT

    def send_kv(s, tile_at):
        for d in range(1, TILES):
            group = peer(d)
            send_kv_tile(s, place_of(group), tile_at, group)
        own_kv(s, tile_at).start()

    def send_q(s):
        for d in range(1, TILES):
            group = peer(d)
            send_q_tile(s, place_of(group), group)
        own_q(s).start()

    def send_half(s):
        for i in range(1, HALF):
            place = lax.rem(chip + i, HALF)
            send_kv_tile(s, place, near_tile, place * WT)
        for i in range(1, HALF):
            place = lax.rem(chip + i, HALF)
            send_q_tile(s, place, place * WT)

        @pl.when(column == 0)
        def _():
            own_kv(s, near_tile).start()
            own_q(s).start()

        @pl.when(column == 1)
        def _():
            send_kv_tile(s, chip, near_tile, sibling)
            send_q_tile(s, chip, sibling)

    def halo_copies(s):
        return [
            remote(
                kv_wide.at[s, 1], kv_wide.at[s, 2 * side],
                halo_send.at[s, side], halo_recv.at[s, side], frame, me,
            )
            for side, frame in enumerate((later, earlier))
        ]

    row_parts = row_heads // HALF
    reach_parts = min(row_parts, 2)

    def part_of(f, part):
        return kv_row.at[f, column, pl.ds(part * HALF, HALF)]

    def staged_part(part):
        return kv_stage.at[pl.ds(row_base + part * HALF, HALF)]

    def row_halo(part):
        return [
            remote(
                staged_part(part), part_of(2 * side, part),
                row_send.at[part, side], row_recv.at[part, side], frame, me,
            )
            for side, frame in enumerate((later, earlier))
        ]

    def to_sibling(f, part):
        return remote(
            staged_part(part) if f == 1 else part_of(f, part), part_of(f, part),
            side_send.at[f, part], side_recv.at[f, part], seq, sibling,
        )

    def own_row():
        rows = pl.ds(row_base, row_heads)
        return [
            pltpu.make_async_copy(kv_stage.at[rows], kv_row.at[1, column], row_sem.at[0]),
            pltpu.make_async_copy(q_stage.at[rows], q_row, row_sem.at[1]),
        ]

    def start_wide_kv(s, carry):
        send_kv(s, wide_tile)
        return carry

    def start_q(s, carry):
        send_q(s)
        return carry

    def start_near(s, carry):
        send_kv(s, near_tile)
        send_q(s)
        return carry

    def forward(s, carry):
        bytes_of(kv_wide.at[s, 1, pl.ds(0, TILES - 1)], kv_recv.at[s]).wait()
        own_kv(s, wide_tile).wait()
        for copy in halo_copies(s):
            copy.start()
        return carry

    send_kv(0, wide_tile)
    if row_heads:
        for copy in row_halo(0):
            copy.start()
    lax.fori_loop(1, wide, start_wide_kv, 0)
    for part in range(row_parts):
        to_sibling(1, part).start()
    if row_heads:
        for copy in own_row():
            copy.start()
    lax.fori_loop(0, wide, start_q, 0)
    if full > wide:
        lax.fori_loop(wide, full, start_near, 0)
    if half:
        send_half(full)
    lax.fori_loop(0, 2, forward, 0)
    if row_heads:
        for side, copy in enumerate(row_halo(0)):
            copy.wait_recv()
            to_sibling(2 * side, 0).start()
    lax.fori_loop(2, wide, forward, 0)
    if reach_parts > 1:
        for copy in row_halo(1):
            copy.start()

    def row_pairs(part, frames):
        def heads(i, carry):
            for j in range(2):
                head = part * HALF + i * 2 + j
                o_row[head] = attend_row(q_row[head], kv_row, frames, head, table)
            return carry

        lax.fori_loop(0, HALF // 2, heads, 0)

    def row_part(part, frames):
        for f in frames:
            to_sibling(f, part).wait_recv()
        row_pairs(part, frames)

    if row_heads:
        for copy in own_row():
            copy.wait()
        row_part(0, (0, 1, 2))
    for part in range(2, row_parts):
        row_part(part, (1,))

    def attend_slot(s, kv_ref, first_frame):
        bytes_of(q_near.at[s, pl.ds(0, TILES - 1)], q_recv.at[s]).wait()
        own_q(s).wait()

        def write(t, tile):
            o_stage[s, t] = tile

        attend(q_near.at[s], kv_ref, (scores_a, scores_b), write, table, s, first_frame)
        position = s * TILES + spot
        for d in range(1, TILES):
            group = peer(d)
            remote(
                o_stage.at[s, group], out.at[position], o_send.at[s], o_recv.at[s], seq, group
            ).start()
        pltpu.make_async_copy(o_stage.at[s, me], out.at[position], own_sem.at[2, s]).start()

    def wide_slot(s, carry):
        for copy in halo_copies(s):
            copy.wait_recv()
        attend_slot(s, kv_wide.at[s], 0)
        return carry

    def near_slot(s, carry):
        bytes_of(kv_near.at[s - wide, 0, pl.ds(0, TILES - 1)], kv_recv.at[s]).wait()
        own_kv(s, near_tile).wait()
        attend_slot(s, kv_near.at[s - wide], 1)
        return carry

    near = slots - wide
    first = max(wide - near, 0)

    def pair(j, carry):
        if half:
            @pl.when((wide + j < full) | (column == 0))
            def _():
                near_slot(wide + j, 0)
        else:
            near_slot(wide + j, 0)
        wide_slot(first + j, 0)
        return carry

    if first:
        lax.fori_loop(0, first, wide_slot, 0)
    if near:
        lax.fori_loop(0, near, pair, 0)

    if reach_parts > 1:
        for side, copy in enumerate(row_halo(1)):
            copy.wait_recv()
            to_sibling(2 * side, 1).start()
        row_part(1, (0, 1, 2))
    if row_heads:
        pltpu.make_async_copy(o_row, out.at[pl.ds(row_base, row_heads)], row_sem.at[2]).start()

    def own_out(s):
        return pltpu.make_async_copy(o_stage.at[s, me], out.at[s * TILES + spot], own_sem.at[2, s])

    def sent_inputs(s, count):
        bytes_of(kv_stage.at[pl.ds(s * TILES, count)], kv_send.at[s]).wait()
        bytes_of(q_stage.at[pl.ds(s * TILES, count)], q_send.at[s]).wait()

    def got_outputs(s, count):
        bytes_of(out.at[pl.ds(s * TILES, count)], o_recv.at[s]).wait()

    def sent_outputs(s):
        own_out(s).wait()
        bytes_of(o_stage.at[s, pl.ds(0, TILES - 1)], o_send.at[s]).wait()

    def finish(s, carry):
        sent_inputs(s, TILES - 1)
        sent_outputs(s)
        got_outputs(s, TILES - 1)
        return carry

    def finish_halo(s, carry):
        for copy in halo_copies(s):
            copy.wait_send()
        return carry

    lax.fori_loop(0, wide, finish_halo, 0)
    for part in range(reach_parts):
        for copy in row_halo(part):
            copy.wait_send()
    for part in range(row_parts):
        for f in (0, 1, 2) if part < 2 else (1,):
            to_sibling(f, part).wait_send()
    if row_heads:
        pltpu.make_async_copy(o_row, out.at[pl.ds(row_base, row_heads)], row_sem.at[2]).wait()
    if half:
        @pl.when(column == 0)
        def _():
            sent_inputs(full, HALF - 1)
            sent_outputs(full)
            got_outputs(full, HALF - 1)

        @pl.when(column == 1)
        def _():
            sent_inputs(full, HALF)
            got_outputs(full, HALF)
    lax.fori_loop(0, full, finish, 0)


def exchange(halves, wide, collective_id, frame_total, table, kv_stage, q_stage):
    slots = (halves + 1) // 2
    near = max(slots - wide, 1)
    row_heads = max(H - halves * HALF, 1)
    vmem = pl.BlockSpec(memory_space=pltpu.VMEM)
    bf16 = jnp.bfloat16
    tile = (TILE, HD)
    dma = pltpu.SemaphoreType.DMA
    scores = pltpu.VMEM((FRAMES * TILES * TILE, WT * TILE), jnp.float32)
    return pl.pallas_call(
        functools.partial(exchange_kernel, halves, wide, frame_total),
        out_shape=pltpu.VMEM((H,) + tile, bf16),
        in_specs=[pl.BlockSpec(memory_space=pltpu.SMEM), vmem, vmem],
        out_specs=vmem,
        scratch_shapes=[
            pltpu.VMEM((wide, FRAMES, TILES, 2) + tile, bf16),
            pltpu.VMEM((near, 1, TILES, 2) + tile, bf16),
            pltpu.VMEM((FRAMES, WT, row_heads, 2) + tile, bf16),
            pltpu.VMEM((slots, TILES) + tile, bf16),
            pltpu.VMEM((row_heads,) + tile, bf16),
            pltpu.VMEM((slots, TILES) + tile, bf16),
            pltpu.VMEM((row_heads,) + tile, bf16),
            scores, scores,
            dma((slots,)), dma((slots,)), dma((slots,)), dma((slots,)),
            dma((wide, 2)), dma((wide, 2)),
            dma((slots,)), dma((slots,)), dma((3, slots)),
            dma((2, 2)), dma((2, 2)),
            dma((FRAMES, ROW_HEADS // HALF)), dma((FRAMES, ROW_HEADS // HALF)),
            dma((3,)),
        ],
        compiler_params=pltpu.CompilerParams(
            collective_id=collective_id, has_side_effects=True, vmem_limit_bytes=40 << 20
        ),
        name=f"exchange_{halves}_{wide}",
    )(table, kv_stage, q_stage)


def power(exponent):
    return jnp.where(exponent > 0, 2.0, jnp.where(exponent < 0, 0.5, 1.0)).astype(jnp.float32)


def prepare_kernel(
    frame_total,
    extents_hbm, q_exp_hbm, k_exp_hbm, v_exp_hbm, q_data, k_data, v_data,
    table, place, plan, kv_stage, q_stage,
    extents, q_exp, k_exp, v_exp, order, q_in, k_in, v_in, in_sem, small_sem,
):
    loads = [
        pltpu.make_async_copy(src, dst, in_sem.at[i])
        for i, (src, dst) in enumerate(((k_data, k_in), (v_data, v_in), (q_data, q_in)))
    ]
    small = [
        pltpu.make_async_copy(src, dst, small_sem.at[i])
        for i, (src, dst) in enumerate(
            (
                (extents_hbm, extents),
                (k_exp_hbm, k_exp),
                (v_exp_hbm, v_exp),
                (q_exp_hbm, q_exp),
            )
        )
    ]
    for load in small + loads:
        load.start()
    for load in small:
        load.wait()

    zero = jnp.int32(0)
    one = jnp.int32(1)

    def flag(condition):
        return jnp.where(condition, one, zero)

    reach = [flag(extents[0, h] >= 1) for h in range(H)]
    flat = [flag(extents[1, h] <= 0) for h in range(H)]
    reaching = sum(reach, zero)
    flat_reaching = sum((r * f for r, f in zip(reach, flat)), zero)
    row_reaching = jnp.minimum(flat_reaching, ROW_REACH)
    row_most = row_reaching + sum(flat, zero) - flat_reaching
    row_count = zero
    for count in range(HALF, ROW_HEADS + 1, HALF):
        fits = reaching - jnp.minimum(row_reaching, count) <= PLANS[0][1] * TILES
        row_count = jnp.where(fits & (row_most >= count), count, row_count)
    row_reaching = jnp.minimum(row_reaching, row_count)
    row_base = H - row_count
    plan[0] = len(PLANS) - 1 - row_count // HALF
    next_reach, next_rest = zero, reaching - row_reaching
    next_row_reach, next_row_rest = zero, row_reaching
    for h in range(H):
        row_index = jnp.where(reach[h] > 0, next_row_reach, next_row_rest)
        row_end = jnp.where(reach[h] > 0, row_reaching, row_count)
        in_row = flat[h] * flag(row_index < row_end)
        outside = 1 - in_row
        other = jnp.where(reach[h] > 0, next_reach, next_rest)
        position = jnp.where(in_row > 0, row_base + row_index, other)
        next_row_reach += in_row * reach[h]
        next_row_rest += in_row * (1 - reach[h])
        next_reach += outside * reach[h]
        next_rest += outside * (1 - reach[h])
        order[position] = h
        place[h] = position
    me = lax.axis_index("head")
    seq = lax.axis_index("seq")
    column = lax.rem(me, WT)
    spot = column * HALF + me // WT

    def within(condition):
        return jnp.where(condition, 0.0, NEG).astype(jnp.float32)

    def beside(head, f):
        inside = (seq + f - 1 >= 0) & (seq + f - 1 < frame_total)
        return within((extents[0, head] >= abs(f - 1)) & inside)

    for s in range(SLOTS):
        head = order[s * TILES + spot]
        entry = s * ENTRIES
        for r in range(HT):
            for t in range(HT):
                table[entry + r * HT + t] = within(extents[1, head] >= abs(r - t))
        for c in range(WT):
            table[entry + HT * HT + c] = within(extents[2, head] >= c)
        for f in range(FRAMES):
            table[entry + HT * HT + WT + f] = beside(head, f)
    for i in range(ROW_HEADS):
        head = order[jnp.minimum(row_base + i, H - 1)]
        entry = ROW_TABLE + i * ROW_ENTRIES
        for c in range(WT):
            table[entry + c] = within(extents[2, head] >= jnp.abs(column - c))
        for f in range(FRAMES):
            table[entry + WT + f] = beside(head, f)


    def scaled(ref, exps, head):
        columns = pl.ds(pl.multiple_of(head * HD, HD), HD)
        return (ref[:, columns].astype(jnp.float32) * power(exps[0, head])).astype(jnp.bfloat16)

    def stage_keys(s, carry):
        for p in range(TILES):
            kv_stage[s * TILES + p, 0] = scaled(k_in, k_exp, order[s * TILES + p])
        return carry

    def stage_values(s, carry):
        for p in range(TILES):
            kv_stage[s * TILES + p, 1] = scaled(v_in, v_exp, order[s * TILES + p]).T
        return carry

    def stage_queries(s, carry):
        for p in range(TILES):
            q_stage[s * TILES + p] = scaled(q_in, q_exp, order[s * TILES + p])
        return carry

    for load, stage in zip(loads, (stage_keys, stage_values, stage_queries)):
        load.wait()
        lax.fori_loop(0, SLOTS, stage, 0)


def prepare(frame_total, extents, q_exp, k_exp, v_exp, q_data, k_data, v_data):
    smem = pl.BlockSpec(memory_space=pltpu.SMEM)
    bf16 = jnp.bfloat16
    kv = (H, 2, TILE, HD)
    q = (H, TILE, HD)
    vmem = pl.BlockSpec(memory_space=pltpu.VMEM)
    whole = pltpu.VMEM((TILE, H * HD), bf16)
    exponents = pltpu.SMEM((1, H), jnp.int32)
    return pl.pallas_call(
        functools.partial(prepare_kernel, frame_total),
        out_shape=(
            pltpu.SMEM((TABLE,), jnp.float32),
            pltpu.SMEM((H,), jnp.int32),
            pltpu.SMEM((1,), jnp.int32),
            pltpu.VMEM(kv, bf16),
            pltpu.VMEM(q, bf16),
        ),
        in_specs=[pl.BlockSpec(memory_space=pltpu.HBM)] * 7,
        out_specs=(smem, smem, smem, vmem, vmem),
        scratch_shapes=[
            pltpu.SMEM((3, H), jnp.int32),
            exponents, exponents, exponents,
            pltpu.SMEM((H,), jnp.int32),
            whole, whole, whole,
            pltpu.SemaphoreType.DMA((3,)),
            pltpu.SemaphoreType.DMA((4,)),
        ],
        compiler_params=pltpu.CompilerParams(vmem_limit_bytes=58 << 20),
        name="prepare",
    )(extents, q_exp, k_exp, v_exp, q_data, k_data, v_data)


def restore_kernel(place, tiles, out, sem):
    for h in range(H):
        pltpu.make_async_copy(tiles.at[place[h]], out.at[:, pl.ds(h * HD, HD)], sem).start()
    bytes_of(out, sem).wait()


def restore(place, tiles):
    return pl.pallas_call(
        restore_kernel,
        out_shape=pltpu.HBM((TILE, H * HD), jnp.bfloat16),
        in_specs=[
            pl.BlockSpec(memory_space=pltpu.SMEM),
            pl.BlockSpec(memory_space=pltpu.VMEM),
        ],
        out_specs=pl.BlockSpec(memory_space=pl.ANY),
        scratch_shapes=[pltpu.SemaphoreType.DMA(())],
        compiler_params=pltpu.CompilerParams(vmem_limit_bytes=40 << 20),
        name="restore",
    )(place, tiles)


def on_device(frame_total, q_data, k_data, v_data, q_exp, k_exp, v_exp, extents):
    table, place, plan, kv_stage, q_stage = prepare(
        frame_total, extents.T, q_exp, k_exp, v_exp, q_data, k_data, v_data
    )

    def branch(index, halves, wide):
        def run(table, place, kv_stage, q_stage):
            tiles = exchange(halves, wide, index, frame_total, table, kv_stage, q_stage)
            return restore(place, tiles)

        return run

    branches = [branch(i, *plan_sizes) for i, plan_sizes in enumerate(PLANS)]
    return lax.switch(plan[0], branches, table, place, kv_stage, q_stage)


def solution(mesh):
    rows = P(("seq", "head"), None)
    return jax.shard_map(
        functools.partial(on_device, mesh.shape["seq"]),
        mesh=mesh,
        in_specs=(rows,) * 6 + (P(),),
        out_specs=rows,
        check_vma=False,
    )
```

```python
import functools
import math

import jax
import jax.numpy as jnp
from jax import lax
from jax.experimental import pallas as pl
from jax.experimental.pallas import tpu as pltpu
from jax.sharding import PartitionSpec as P

H = 48
HD = 128
TILE = 128
HT = 4
WT = 2
TILES = HT * WT
HALF = TILES // 2
FRAMES = 3
NEG = -1e30
LOG2_SCALE = math.log2(math.e) / math.sqrt(HD)
MESH = pl.DeviceIdType.MESH

PLANS = ((9, 3), (10, 3), (11, 3), (12, 6))
ROW_HEADS = 12
ROW_REACH = 8

SLOTS = H // TILES
ENTRIES = HT * HT + WT + FRAMES
ROW_TABLE = SLOTS * ENTRIES
ROW_ENTRIES = WT + FRAMES
TABLE = ROW_TABLE + ROW_HEADS * ROW_ENTRIES


def bytes_of(ref, sem):
    return pltpu.make_async_copy(ref, ref, sem)


def block_max(s):
    return jnp.max(s.reshape(s.shape[0] // 8, 8, s.shape[1]), axis=0)


def attend(q_ref, kv_ref, score_refs, write, send, table, slot, first_frame):
    frames = kv_ref.shape[0]
    entry = slot * ENTRIES

    def biases(row):
        rows = [table[entry + row * HT + r] for r in range(HT)]
        columns = [table[entry + HT * HT + c] for c in range(WT)]
        beside = [table[entry + HT * HT + WT + first_frame + f] for f in range(frames)]
        return lambda f, t, u: rows[t // WT] + columns[abs(t % WT - u)] + beside[f]

    def score(row, s_ref):
        bias = biases(row)
        queries = q_ref[pl.ds(row * WT, WT)].reshape(WT * TILE, HD)
        peak = [None] * WT
        for f in range(frames):
            for t in range(0, TILES, WT):
                keys = kv_ref[f, t : t + WT, 0].reshape(WT * TILE, HD)
                s = lax.dot_general(
                    keys, queries, (((1,), (1,)), ((), ())), preferred_element_type=jnp.float32
                )
                base = (f * TILES + t) * TILE
                s_ref[base : base + WT * TILE, :] = s
                for j in range(WT):
                    for u in range(WT):
                        block = s[j * TILE : (j + 1) * TILE, u * TILE : (u + 1) * TILE]
                        top = block_max(block) + bias(f, t + j, u)
                        peak[u] = top if peak[u] is None else jnp.maximum(peak[u], top)
        return [jnp.max(p, axis=0, keepdims=True) * LOG2_SCALE for p in peak]

    def combine(row, s_ref, peak):
        bias = biases(row)
        ones = jnp.ones((16, WT * TILE), jnp.bfloat16)
        total = None
        for f in range(frames):
            for t in range(0, TILES, WT):
                base = (f * TILES + t) * TILE
                columns = []
                for u in range(WT):
                    parts = []
                    for j in range(WT):
                        s = s_ref[base + j * TILE : base + (j + 1) * TILE, u * TILE : (u + 1) * TILE]
                        shift = bias(f, t + j, u) - peak[u]
                        parts.append(jnp.exp2(s * LOG2_SCALE + shift).astype(jnp.bfloat16))
                    columns.append(jnp.concatenate(parts, axis=0))
                weights = jnp.concatenate(columns, axis=1)
                values = jnp.concatenate([kv_ref[f, t + j, 1] for j in range(WT)], axis=1)
                values = jnp.concatenate([values, ones], axis=0)
                part = jnp.dot(values, weights, preferred_element_type=jnp.float32)
                total = part if total is None else total + part
        out = total[:HD] * (1.0 / total[HD : HD + 1])
        for u in range(WT):
            write(row * WT + u, out[:, u * TILE : (u + 1) * TILE].T.astype(jnp.bfloat16))

    def rows(i, carry):
        at = [i * 2 + j for j in range(2)]
        peaks = [score(r, s_ref) for r, s_ref in zip(at, score_refs)]
        for r, s_ref, peak in zip(at, score_refs, peaks):
            combine(r, s_ref, peak)
        for r in at:
            for u in range(WT):
                send(r * WT + u)
        return carry

    lax.fori_loop(0, HT // 2, rows, 0)


def attend_row(queries, kv_ref, frames, head, table):
    entry = ROW_TABLE + head * ROW_ENTRIES
    columns = [table[entry + c] for c in range(WT)]
    blocks = [(f, c, columns[c] + table[entry + WT + f]) for f in frames for c in range(WT)]
    scores = []
    peak = None
    for f, c, bias in blocks:
        s = lax.dot_general(
            kv_ref[f, c, head, 0], queries, (((1,), (1,)), ((), ())), preferred_element_type=jnp.float32
        )
        scores.append(s)
        top = block_max(s) + bias
        peak = top if peak is None else jnp.maximum(peak, top)
    peak = jnp.max(peak, axis=0, keepdims=True) * LOG2_SCALE
    weights = jnp.concatenate(
        [jnp.exp2(s * LOG2_SCALE + (bias - peak)) for s, (_, _, bias) in zip(scores, blocks)], axis=0
    ).astype(jnp.bfloat16)
    values = jnp.concatenate([kv_ref[f, c, head, 1] for f, c, _ in blocks], axis=1)
    values = jnp.concatenate([values, jnp.ones((16, values.shape[1]), jnp.bfloat16)], axis=0)
    total = jnp.dot(values, weights, preferred_element_type=jnp.float32)
    return (total[:HD] * (1.0 / total[HD : HD + 1])).T.astype(jnp.bfloat16)


def exchange_kernel(
    halves, wide, frame_total,
    table, kv_stage, q_stage,
    out,
    kv_wide, kv_near, kv_row, q_near, q_row, o_stage, o_row, scores_a, scores_b,
    kv_send, kv_recv, q_send, q_recv, halo_send, halo_recv, o_send, o_recv, own_sem,
    row_send, row_recv, side_send, side_recv, row_sem,
):
    full, half = halves // 2, halves % 2
    slots = full + half
    row_base = halves * HALF
    row_heads = H - row_base
    me = lax.axis_index("head")
    seq = lax.axis_index("seq")
    later = lax.rem(seq + 1, frame_total)
    earlier = lax.rem(seq + frame_total - 1, frame_total)
    column = lax.rem(me, WT)
    chip = me // WT
    sibling = me + 1 - 2 * column
    spot = column * HALF + chip

    def peer(d):
        return lax.rem(me + d, TILES)

    barrier = pltpu.get_barrier_semaphore()
    for d in range(1, TILES):
        pl.semaphore_signal(barrier, inc=1, device_id=(seq, peer(d)), device_id_type=MESH)
    for frame in (later, earlier):
        pl.semaphore_signal(barrier, inc=1, device_id=(frame, me), device_id_type=MESH)
    pl.semaphore_wait(barrier, TILES - 1 + 2)

    def remote(src, dst, send, recv, frame, group):
        return pltpu.make_async_remote_copy(
            src_ref=src, dst_ref=dst, send_sem=send, recv_sem=recv,
            device_id=(frame, group), device_id_type=MESH,
        )

    def wide_tile(s, t):
        return kv_wide.at[s, 1, t]

    def near_tile(s, t):
        return kv_near.at[s - wide, 0, t]

    def send_kv_tile(s, place, tile_at, group):
        src = kv_stage.at[s * TILES + place]
        remote(src, tile_at(s, me), kv_send.at[s], kv_recv.at[s], seq, group).start()

    def send_q_tile(s, place, group):
        src = q_stage.at[s * TILES + place]
        remote(src, q_near.at[s, me], q_send.at[s], q_recv.at[s], seq, group).start()

    def own_kv(s, tile_at):
        return pltpu.make_async_copy(kv_stage.at[s * TILES + spot], tile_at(s, me), own_sem.at[0, s])

    def own_q(s):
        return pltpu.make_async_copy(q_stage.at[s * TILES + spot], q_near.at[s, me], own_sem.at[1, s])

    def place_of(group):
        return lax.rem(group, WT) * HALF + group // WT

    def send_kv(s, tile_at):
        for d in range(1, TILES):
            group = peer(d)
            send_kv_tile(s, place_of(group), tile_at, group)
        own_kv(s, tile_at).start()

    def send_q(s):
        for d in range(1, TILES):
            group = peer(d)
            send_q_tile(s, place_of(group), group)
        own_q(s).start()

    def send_half(s):
        for i in range(1, HALF):
            place = lax.rem(chip + i, HALF)
            send_kv_tile(s, place, near_tile, place * WT)
        for i in range(1, HALF):
            place = lax.rem(chip + i, HALF)
            send_q_tile(s, place, place * WT)

        @pl.when(column == 0)
        def _():
            own_kv(s, near_tile).start()
            own_q(s).start()

        @pl.when(column == 1)
        def _():
            send_kv_tile(s, chip, near_tile, sibling)
            send_q_tile(s, chip, sibling)

    def halo_copies(s):
        return [
            remote(
                kv_wide.at[s, 1], kv_wide.at[s, 2 * side],
                halo_send.at[s, side], halo_recv.at[s, side], frame, me,
            )
            for side, frame in enumerate((later, earlier))
        ]

    row_parts = row_heads // HALF
    reach_parts = min(row_parts, 2)

    def part_of(f, part):
        return kv_row.at[f, column, pl.ds(part * HALF, HALF)]

    def staged_part(part):
        return kv_stage.at[pl.ds(row_base + part * HALF, HALF)]

    def row_halo(part):
        return [
            remote(
                staged_part(part), part_of(2 * side, part),
                row_send.at[part, side], row_recv.at[part, side], frame, me,
            )
            for side, frame in enumerate((later, earlier))
        ]

    def to_sibling(f, part):
        return remote(
            staged_part(part) if f == 1 else part_of(f, part), part_of(f, part),
            side_send.at[f, part], side_recv.at[f, part], seq, sibling,
        )

    def own_row():
        rows = pl.ds(row_base, row_heads)
        return [
            pltpu.make_async_copy(kv_stage.at[rows], kv_row.at[1, column], row_sem.at[0]),
            pltpu.make_async_copy(q_stage.at[rows], q_row, row_sem.at[1]),
        ]

    def start_wide_kv(s, carry):
        send_kv(s, wide_tile)
        return carry

    def start_q(s, carry):
        send_q(s)
        return carry

    def start_near(s, carry):
        send_kv(s, near_tile)
        send_q(s)
        return carry

    def forward(s, carry):
        bytes_of(kv_wide.at[s, 1, pl.ds(0, TILES - 1)], kv_recv.at[s]).wait()
        own_kv(s, wide_tile).wait()
        for copy in halo_copies(s):
            copy.start()
        return carry

    send_kv(0, wide_tile)
    if row_heads:
        for copy in row_halo(0):
            copy.start()
    lax.fori_loop(1, wide, start_wide_kv, 0)
    for part in range(row_parts):
        to_sibling(1, part).start()
    if row_heads:
        for copy in own_row():
            copy.start()
    lax.fori_loop(0, wide, start_q, 0)
    if full > wide:
        lax.fori_loop(wide, full, start_near, 0)
    if half:
        send_half(full)
    lax.fori_loop(0, 2, forward, 0)
    if row_heads:
        for side, copy in enumerate(row_halo(0)):
            copy.wait_recv()
            to_sibling(2 * side, 0).start()
    lax.fori_loop(2, wide, forward, 0)
    if reach_parts > 1:
        for copy in row_halo(1):
            copy.start()

    def row_pairs(part, frames):
        def heads(i, carry):
            for j in range(2):
                head = part * HALF + i * 2 + j
                o_row[head] = attend_row(q_row[head], kv_row, frames, head, table)
            return carry

        lax.fori_loop(0, HALF // 2, heads, 0)

    def row_part(part, frames):
        for f in frames:
            to_sibling(f, part).wait_recv()
        row_pairs(part, frames)

    if row_heads:
        for copy in own_row():
            copy.wait()
        row_part(0, (0, 1, 2))
    for part in range(2, row_parts):
        row_part(part, (1,))

    def attend_slot(s, kv_ref, first_frame):
        bytes_of(q_near.at[s, pl.ds(0, TILES - 1)], q_recv.at[s]).wait()
        own_q(s).wait()

        def write(t, tile):
            o_stage[s, t] = tile

        position = s * TILES + spot

        def send(t):
            @pl.when(t == me)
            def _():
                pltpu.make_async_copy(o_stage.at[s, t], out.at[position], own_sem.at[2, s]).start()

            @pl.when(t != me)
            def _():
                remote(
                    o_stage.at[s, t], out.at[position], o_send.at[s], o_recv.at[s], seq, t
                ).start()

        attend(q_near.at[s], kv_ref, (scores_a, scores_b), write, send, table, s, first_frame)

    def wide_slot(s, carry):
        for copy in halo_copies(s):
            copy.wait_recv()
        attend_slot(s, kv_wide.at[s], 0)
        return carry

    def near_slot(s, carry):
        bytes_of(kv_near.at[s - wide, 0, pl.ds(0, TILES - 1)], kv_recv.at[s]).wait()
        own_kv(s, near_tile).wait()
        attend_slot(s, kv_near.at[s - wide], 1)
        return carry

    near = slots - wide
    first = max(wide - near, 0)

    def pair(j, carry):
        if half:
            @pl.when((wide + j < full) | (column == 0))
            def _():
                near_slot(wide + j, 0)
        else:
            near_slot(wide + j, 0)
        wide_slot(first + j, 0)
        return carry

    if first:
        lax.fori_loop(0, first, wide_slot, 0)
    if near:
        lax.fori_loop(0, near, pair, 0)

    if reach_parts > 1:
        for side, copy in enumerate(row_halo(1)):
            copy.wait_recv()
            to_sibling(2 * side, 1).start()
        row_part(1, (0, 1, 2))
    if row_heads:
        pltpu.make_async_copy(o_row, out.at[pl.ds(row_base, row_heads)], row_sem.at[2]).start()

    def own_out(s):
        return pltpu.make_async_copy(o_stage.at[s, me], out.at[s * TILES + spot], own_sem.at[2, s])

    def sent_inputs(s, count):
        bytes_of(kv_stage.at[pl.ds(s * TILES, count)], kv_send.at[s]).wait()
        bytes_of(q_stage.at[pl.ds(s * TILES, count)], q_send.at[s]).wait()

    def got_outputs(s, count):
        bytes_of(out.at[pl.ds(s * TILES, count)], o_recv.at[s]).wait()

    def sent_outputs(s):
        own_out(s).wait()
        bytes_of(o_stage.at[s, pl.ds(0, TILES - 1)], o_send.at[s]).wait()

    def finish(s, carry):
        sent_inputs(s, TILES - 1)
        sent_outputs(s)
        got_outputs(s, TILES - 1)
        return carry

    def finish_halo(s, carry):
        for copy in halo_copies(s):
            copy.wait_send()
        return carry

    lax.fori_loop(0, wide, finish_halo, 0)
    for part in range(reach_parts):
        for copy in row_halo(part):
            copy.wait_send()
    for part in range(row_parts):
        for f in (0, 1, 2) if part < 2 else (1,):
            to_sibling(f, part).wait_send()
    if row_heads:
        pltpu.make_async_copy(o_row, out.at[pl.ds(row_base, row_heads)], row_sem.at[2]).wait()
    if half:
        @pl.when(column == 0)
        def _():
            sent_inputs(full, HALF - 1)
            sent_outputs(full)
            got_outputs(full, HALF - 1)

        @pl.when(column == 1)
        def _():
            sent_inputs(full, HALF)
            got_outputs(full, HALF)
    lax.fori_loop(0, full, finish, 0)


def exchange(halves, wide, collective_id, frame_total, table, kv_stage, q_stage):
    slots = (halves + 1) // 2
    near = max(slots - wide, 1)
    row_heads = max(H - halves * HALF, 1)
    vmem = pl.BlockSpec(memory_space=pltpu.VMEM)
    bf16 = jnp.bfloat16
    tile = (TILE, HD)
    dma = pltpu.SemaphoreType.DMA
    scores = pltpu.VMEM((FRAMES * TILES * TILE, WT * TILE), jnp.float32)
    return pl.pallas_call(
        functools.partial(exchange_kernel, halves, wide, frame_total),
        out_shape=pltpu.VMEM((H,) + tile, bf16),
        in_specs=[pl.BlockSpec(memory_space=pltpu.SMEM), vmem, vmem],
        out_specs=vmem,
        scratch_shapes=[
            pltpu.VMEM((wide, FRAMES, TILES, 2) + tile, bf16),
            pltpu.VMEM((near, 1, TILES, 2) + tile, bf16),
            pltpu.VMEM((FRAMES, WT, row_heads, 2) + tile, bf16),
            pltpu.VMEM((slots, TILES) + tile, bf16),
            pltpu.VMEM((row_heads,) + tile, bf16),
            pltpu.VMEM((slots, TILES) + tile, bf16),
            pltpu.VMEM((row_heads,) + tile, bf16),
            scores, scores,
            dma((slots,)), dma((slots,)), dma((slots,)), dma((slots,)),
            dma((wide, 2)), dma((wide, 2)),
            dma((slots,)), dma((slots,)), dma((3, slots)),
            dma((2, 2)), dma((2, 2)),
            dma((FRAMES, ROW_HEADS // HALF)), dma((FRAMES, ROW_HEADS // HALF)),
            dma((3,)),
        ],
        compiler_params=pltpu.CompilerParams(
            collective_id=collective_id, has_side_effects=True, vmem_limit_bytes=40 << 20
        ),
        name=f"exchange_{halves}_{wide}",
    )(table, kv_stage, q_stage)


def power(exponent):
    return jnp.where(exponent > 0, 2.0, jnp.where(exponent < 0, 0.5, 1.0)).astype(jnp.float32)


def prepare_kernel(
    frame_total,
    extents_hbm, q_exp_hbm, k_exp_hbm, v_exp_hbm, q_data, k_data, v_data,
    table, place, plan, kv_stage, q_stage,
    extents, q_exp, k_exp, v_exp, order, q_in, k_in, v_in, in_sem, small_sem,
):
    loads = [
        pltpu.make_async_copy(src, dst, in_sem.at[i])
        for i, (src, dst) in enumerate(((k_data, k_in), (v_data, v_in), (q_data, q_in)))
    ]
    small = [
        pltpu.make_async_copy(src, dst, small_sem.at[i])
        for i, (src, dst) in enumerate(
            (
                (extents_hbm, extents),
                (k_exp_hbm, k_exp),
                (v_exp_hbm, v_exp),
                (q_exp_hbm, q_exp),
            )
        )
    ]
    for load in small + loads:
        load.start()
    for load in small:
        load.wait()

    zero = jnp.int32(0)
    one = jnp.int32(1)

    def flag(condition):
        return jnp.where(condition, one, zero)

    reach = [flag(extents[0, h] >= 1) for h in range(H)]
    flat = [flag(extents[1, h] <= 0) for h in range(H)]
    reaching = sum(reach, zero)
    flat_reaching = sum((r * f for r, f in zip(reach, flat)), zero)
    row_reaching = jnp.minimum(flat_reaching, ROW_REACH)
    row_most = row_reaching + sum(flat, zero) - flat_reaching
    row_count = zero
    for count in range(HALF, ROW_HEADS + 1, HALF):
        fits = reaching - jnp.minimum(row_reaching, count) <= PLANS[0][1] * TILES
        row_count = jnp.where(fits & (row_most >= count), count, row_count)
    row_reaching = jnp.minimum(row_reaching, row_count)
    row_base = H - row_count
    plan[0] = len(PLANS) - 1 - row_count // HALF
    next_reach, next_rest = zero, reaching - row_reaching
    next_row_reach, next_row_rest = zero, row_reaching
    for h in range(H):
        row_index = jnp.where(reach[h] > 0, next_row_reach, next_row_rest)
        row_end = jnp.where(reach[h] > 0, row_reaching, row_count)
        in_row = flat[h] * flag(row_index < row_end)
        outside = 1 - in_row
        other = jnp.where(reach[h] > 0, next_reach, next_rest)
        position = jnp.where(in_row > 0, row_base + row_index, other)
        next_row_reach += in_row * reach[h]
        next_row_rest += in_row * (1 - reach[h])
        next_reach += outside * reach[h]
        next_rest += outside * (1 - reach[h])
        order[position] = h
        place[h] = position
    me = lax.axis_index("head")
    seq = lax.axis_index("seq")
    column = lax.rem(me, WT)
    spot = column * HALF + me // WT

    def within(condition):
        return jnp.where(condition, 0.0, NEG).astype(jnp.float32)

    def beside(head, f):
        inside = (seq + f - 1 >= 0) & (seq + f - 1 < frame_total)
        return within((extents[0, head] >= abs(f - 1)) & inside)

    for s in range(SLOTS):
        head = order[s * TILES + spot]
        entry = s * ENTRIES
        for r in range(HT):
            for t in range(HT):
                table[entry + r * HT + t] = within(extents[1, head] >= abs(r - t))
        for c in range(WT):
            table[entry + HT * HT + c] = within(extents[2, head] >= c)
        for f in range(FRAMES):
            table[entry + HT * HT + WT + f] = beside(head, f)
    for i in range(ROW_HEADS):
        head = order[jnp.minimum(row_base + i, H - 1)]
        entry = ROW_TABLE + i * ROW_ENTRIES
        for c in range(WT):
            table[entry + c] = within(extents[2, head] >= jnp.abs(column - c))
        for f in range(FRAMES):
            table[entry + WT + f] = beside(head, f)


    def scaled(ref, exps, head):
        columns = pl.ds(pl.multiple_of(head * HD, HD), HD)
        return (ref[:, columns].astype(jnp.float32) * power(exps[0, head])).astype(jnp.bfloat16)

    def stage_keys(s, carry):
        for p in range(TILES):
            kv_stage[s * TILES + p, 0] = scaled(k_in, k_exp, order[s * TILES + p])
        return carry

    def stage_values(s, carry):
        for p in range(TILES):
            kv_stage[s * TILES + p, 1] = scaled(v_in, v_exp, order[s * TILES + p]).T
        return carry

    def stage_queries(s, carry):
        for p in range(TILES):
            q_stage[s * TILES + p] = scaled(q_in, q_exp, order[s * TILES + p])
        return carry

    for load, stage in zip(loads, (stage_keys, stage_values, stage_queries)):
        load.wait()
        lax.fori_loop(0, SLOTS, stage, 0)


def prepare(frame_total, extents, q_exp, k_exp, v_exp, q_data, k_data, v_data):
    smem = pl.BlockSpec(memory_space=pltpu.SMEM)
    bf16 = jnp.bfloat16
    kv = (H, 2, TILE, HD)
    q = (H, TILE, HD)
    vmem = pl.BlockSpec(memory_space=pltpu.VMEM)
    whole = pltpu.VMEM((TILE, H * HD), bf16)
    exponents = pltpu.SMEM((1, H), jnp.int32)
    return pl.pallas_call(
        functools.partial(prepare_kernel, frame_total),
        out_shape=(
            pltpu.SMEM((TABLE,), jnp.float32),
            pltpu.SMEM((H,), jnp.int32),
            pltpu.SMEM((1,), jnp.int32),
            pltpu.VMEM(kv, bf16),
            pltpu.VMEM(q, bf16),
        ),
        in_specs=[pl.BlockSpec(memory_space=pltpu.HBM)] * 7,
        out_specs=(smem, smem, smem, vmem, vmem),
        scratch_shapes=[
            pltpu.SMEM((3, H), jnp.int32),
            exponents, exponents, exponents,
            pltpu.SMEM((H,), jnp.int32),
            whole, whole, whole,
            pltpu.SemaphoreType.DMA((3,)),
            pltpu.SemaphoreType.DMA((4,)),
        ],
        compiler_params=pltpu.CompilerParams(vmem_limit_bytes=58 << 20),
        name="prepare",
    )(extents, q_exp, k_exp, v_exp, q_data, k_data, v_data)


def restore_kernel(place, tiles, out, sem):
    for h in range(H):
        pltpu.make_async_copy(tiles.at[place[h]], out.at[:, pl.ds(h * HD, HD)], sem).start()
    bytes_of(out, sem).wait()


def restore(place, tiles):
    return pl.pallas_call(
        restore_kernel,
        out_shape=pltpu.HBM((TILE, H * HD), jnp.bfloat16),
        in_specs=[
            pl.BlockSpec(memory_space=pltpu.SMEM),
            pl.BlockSpec(memory_space=pltpu.VMEM),
        ],
        out_specs=pl.BlockSpec(memory_space=pl.ANY),
        scratch_shapes=[pltpu.SemaphoreType.DMA(())],
        compiler_params=pltpu.CompilerParams(vmem_limit_bytes=40 << 20),
        name="restore",
    )(place, tiles)


def on_device(frame_total, q_data, k_data, v_data, q_exp, k_exp, v_exp, extents):
    table, place, plan, kv_stage, q_stage = prepare(
        frame_total, extents.T, q_exp, k_exp, v_exp, q_data, k_data, v_data
    )

    def branch(index, halves, wide):
        def run(table, place, kv_stage, q_stage):
            tiles = exchange(halves, wide, index, frame_total, table, kv_stage, q_stage)
            return restore(place, tiles)

        return run

    branches = [branch(i, *plan_sizes) for i, plan_sizes in enumerate(PLANS)]
    return lax.switch(plan[0], branches, table, place, kv_stage, q_stage)


def solution(mesh):
    rows = P(("seq", "head"), None)
    return jax.shard_map(
        functools.partial(on_device, mesh.shape["seq"]),
        mesh=mesh,
        in_specs=(rows,) * 6 + (P(),),
        out_specs=rows,
        check_vma=False,
    )
```

```python
import functools
import math

import jax
import jax.numpy as jnp
from jax import lax
from jax.experimental import pallas as pl
from jax.experimental.pallas import tpu as pltpu
from jax.sharding import PartitionSpec as P

H = 48
HD = 128
TILE = 128
HT = 4
WT = 2
TILES = HT * WT
HALF = TILES // 2
FRAMES = 3
NEG = -1e30
LOG2_SCALE = math.log2(math.e) / math.sqrt(HD)
MESH = pl.DeviceIdType.MESH

PLANS = ((9, 3), (10, 3), (11, 3), (12, 6))
ROW_HEADS = 12
ROW_REACH = 8

SLOTS = H // TILES
ENTRIES = HT * HT + WT + FRAMES
ROW_TABLE = SLOTS * ENTRIES
ROW_ENTRIES = WT + FRAMES
TABLE = ROW_TABLE + ROW_HEADS * ROW_ENTRIES


def bytes_of(ref, sem):
    return pltpu.make_async_copy(ref, ref, sem)


def block_max(s):
    return jnp.max(s.reshape(s.shape[0] // 8, 8, s.shape[1]), axis=0)


def attend(q_ref, kv_ref, score_refs, write, send, table, slot, first_frame):
    frames = kv_ref.shape[0]
    entry = slot * ENTRIES

    def biases(row):
        rows = [table[entry + row * HT + r] for r in range(HT)]
        columns = [table[entry + HT * HT + c] for c in range(WT)]
        beside = [table[entry + HT * HT + WT + first_frame + f] for f in range(frames)]
        return lambda f, t, u: rows[t // WT] + columns[abs(t % WT - u)] + beside[f]

    def score(row, s_ref):
        bias = biases(row)
        queries = q_ref[pl.ds(row * WT, WT)].reshape(WT * TILE, HD)
        peak = [None] * WT
        for f in range(frames):
            for t in range(0, TILES, WT):
                keys = kv_ref[f, t : t + WT, 0].reshape(WT * TILE, HD)
                s = lax.dot_general(
                    keys, queries, (((1,), (1,)), ((), ())), preferred_element_type=jnp.float32
                )
                base = (f * TILES + t) * TILE
                s_ref[base : base + WT * TILE, :] = s
                for j in range(WT):
                    for u in range(WT):
                        block = s[j * TILE : (j + 1) * TILE, u * TILE : (u + 1) * TILE]
                        top = block_max(block) + bias(f, t + j, u)
                        peak[u] = top if peak[u] is None else jnp.maximum(peak[u], top)
        return [jnp.max(p, axis=0, keepdims=True) * LOG2_SCALE for p in peak]

    def combine(row, s_ref, peak):
        bias = biases(row)
        ones = jnp.ones((16, WT * TILE), jnp.bfloat16)
        total = None
        for f in range(frames):
            for t in range(0, TILES, WT):
                base = (f * TILES + t) * TILE
                columns = []
                for u in range(WT):
                    parts = []
                    for j in range(WT):
                        s = s_ref[base + j * TILE : base + (j + 1) * TILE, u * TILE : (u + 1) * TILE]
                        shift = bias(f, t + j, u) - peak[u]
                        parts.append(jnp.exp2(s * LOG2_SCALE + shift).astype(jnp.bfloat16))
                    columns.append(jnp.concatenate(parts, axis=0))
                weights = jnp.concatenate(columns, axis=1)
                values = jnp.concatenate([kv_ref[f, t + j, 1] for j in range(WT)], axis=1)
                values = jnp.concatenate([values, ones], axis=0)
                part = jnp.dot(values, weights, preferred_element_type=jnp.float32)
                total = part if total is None else total + part
        out = total[:HD] * (1.0 / total[HD : HD + 1])
        for u in range(WT):
            write(row * WT + u, out[:, u * TILE : (u + 1) * TILE].T.astype(jnp.bfloat16))

    def rows(i, carry):
        at = [i * 2 + j for j in range(2)]
        peaks = [score(r, s_ref) for r, s_ref in zip(at, score_refs)]
        for r, s_ref, peak in zip(at, score_refs, peaks):
            combine(r, s_ref, peak)
        for r in at:
            for u in range(WT):
                send(r * WT + u)
        return carry

    lax.fori_loop(0, HT // 2, rows, 0)


def attend_row(queries, kv_ref, frames, head, table):
    entry = ROW_TABLE + head * ROW_ENTRIES
    columns = [table[entry + c] for c in range(WT)]
    blocks = [(f, c, columns[c] + table[entry + WT + f]) for f in frames for c in range(WT)]
    scores = []
    peak = None
    for f, c, bias in blocks:
        s = lax.dot_general(
            kv_ref[f, c, head, 0], queries, (((1,), (1,)), ((), ())), preferred_element_type=jnp.float32
        )
        scores.append(s)
        top = block_max(s) + bias
        peak = top if peak is None else jnp.maximum(peak, top)
    peak = jnp.max(peak, axis=0, keepdims=True) * LOG2_SCALE
    weights = jnp.concatenate(
        [jnp.exp2(s * LOG2_SCALE + (bias - peak)) for s, (_, _, bias) in zip(scores, blocks)], axis=0
    ).astype(jnp.bfloat16)
    values = jnp.concatenate([kv_ref[f, c, head, 1] for f, c, _ in blocks], axis=1)
    values = jnp.concatenate([values, jnp.ones((16, values.shape[1]), jnp.bfloat16)], axis=0)
    total = jnp.dot(values, weights, preferred_element_type=jnp.float32)
    return (total[:HD] * (1.0 / total[HD : HD + 1])).T.astype(jnp.bfloat16)


def exchange_kernel(
    halves, wide, frame_total,
    table, kv_stage, q_stage,
    out,
    kv_wide, kv_near, kv_row, q_near, q_row, o_stage, o_row, scores_a, scores_b,
    kv_send, kv_recv, q_send, q_recv, halo_send, halo_recv, o_send, o_recv, own_sem,
    row_send, row_recv, side_send, side_recv, row_sem,
):
    full, half = halves // 2, halves % 2
    slots = full + half
    row_base = halves * HALF
    row_heads = H - row_base
    me = lax.axis_index("head")
    seq = lax.axis_index("seq")
    later = lax.rem(seq + 1, frame_total)
    earlier = lax.rem(seq + frame_total - 1, frame_total)
    column = lax.rem(me, WT)
    chip = me // WT
    sibling = me + 1 - 2 * column
    spot = column * HALF + chip

    def peer(d):
        return lax.rem(me + d, TILES)

    barrier = pltpu.get_barrier_semaphore()
    for d in range(1, TILES):
        pl.semaphore_signal(barrier, inc=1, device_id=(seq, peer(d)), device_id_type=MESH)
    for frame in (later, earlier):
        pl.semaphore_signal(barrier, inc=1, device_id=(frame, me), device_id_type=MESH)
    pl.semaphore_wait(barrier, TILES - 1 + 2)

    def remote(src, dst, send, recv, frame, group):
        return pltpu.make_async_remote_copy(
            src_ref=src, dst_ref=dst, send_sem=send, recv_sem=recv,
            device_id=(frame, group), device_id_type=MESH,
        )

    def wide_tile(s, t):
        return kv_wide.at[s, 1, t]

    def near_tile(s, t):
        return kv_near.at[s - wide, 0, t]

    def send_kv_tile(s, place, tile_at, group):
        src = kv_stage.at[s * TILES + place]
        remote(src, tile_at(s, me), kv_send.at[s], kv_recv.at[s], seq, group).start()

    def send_q_tile(s, place, group):
        src = q_stage.at[s, place]
        remote(src, q_near.at[s, me], q_send.at[s], q_recv.at[s], seq, group).start()

    def own_kv(s, tile_at):
        return pltpu.make_async_copy(kv_stage.at[s * TILES + spot], tile_at(s, me), own_sem.at[0, s])

    def own_q(s):
        return pltpu.make_async_copy(q_stage.at[s, spot], q_near.at[s, me], own_sem.at[1, s])

    def place_of(group):
        return lax.rem(group, WT) * HALF + group // WT

    def send_kv(s, tile_at):
        for d in range(1, TILES):
            group = peer(d)
            send_kv_tile(s, place_of(group), tile_at, group)
        own_kv(s, tile_at).start()

    def send_q(s):
        for d in range(1, TILES):
            group = peer(d)
            send_q_tile(s, place_of(group), group)
        own_q(s).start()

    def send_half(s):
        for i in range(1, HALF):
            place = lax.rem(chip + i, HALF)
            send_kv_tile(s, place, near_tile, place * WT)
        for i in range(1, HALF):
            place = lax.rem(chip + i, HALF)
            send_q_tile(s, place, place * WT)

        @pl.when(column == 0)
        def _():
            own_kv(s, near_tile).start()
            own_q(s).start()

        @pl.when(column == 1)
        def _():
            send_kv_tile(s, chip, near_tile, sibling)
            send_q_tile(s, chip, sibling)

    def halo_copies(s):
        return [
            remote(
                kv_wide.at[s, 1], kv_wide.at[s, 2 * side],
                halo_send.at[s, side], halo_recv.at[s, side], frame, me,
            )
            for side, frame in enumerate((later, earlier))
        ]

    row_parts = row_heads // HALF
    reach_parts = min(row_parts, 2)

    def part_of(f, part):
        return kv_row.at[f, column, pl.ds(part * HALF, HALF)]

    def staged_part(part):
        return kv_stage.at[pl.ds(row_base + part * HALF, HALF)]

    def row_halo(part):
        return [
            remote(
                staged_part(part), part_of(2 * side, part),
                row_send.at[part, side], row_recv.at[part, side], frame, me,
            )
            for side, frame in enumerate((later, earlier))
        ]

    def to_sibling(f, part):
        return remote(
            staged_part(part) if f == 1 else part_of(f, part), part_of(f, part),
            side_send.at[f, part], side_recv.at[f, part], seq, sibling,
        )

    def own_row():
        rows = pl.ds(row_base, row_heads)
        return pltpu.make_async_copy(kv_stage.at[rows], kv_row.at[1, column], row_sem.at[0])

    def own_row_q(part):
        slot, start = divmod(row_base + part * HALF, TILES)
        src = q_stage.at[slot, pl.ds(start, HALF)]
        return pltpu.make_async_copy(src, q_row.at[pl.ds(part * HALF, HALF)], row_sem.at[1])

    wide_slots = pl.ds(0, wide)

    def send_wide_q():
        for d in range(1, TILES):
            group = peer(d)
            remote(
                q_stage.at[wide_slots, place_of(group)], q_near.at[wide_slots, me],
                q_send.at[0], q_recv.at[0], seq, group,
            ).start()
        for s in range(wide):
            own_q(s).start()

    def start_wide_kv(s, carry):
        send_kv(s, wide_tile)
        return carry

    def start_near(s, carry):
        send_kv(s, near_tile)
        send_q(s)
        return carry

    def forward(s, carry):
        bytes_of(kv_wide.at[s, 1, pl.ds(0, TILES - 1)], kv_recv.at[s]).wait()
        own_kv(s, wide_tile).wait()
        for copy in halo_copies(s):
            copy.start()
        return carry

    send_kv(0, wide_tile)
    if row_heads:
        for copy in row_halo(0):
            copy.start()
    lax.fori_loop(1, wide, start_wide_kv, 0)
    for part in range(row_parts):
        to_sibling(1, part).start()
    if row_heads:
        own_row().start()
        for part in range(row_parts):
            own_row_q(part).start()
    send_wide_q()
    if full > wide:
        lax.fori_loop(wide, full, start_near, 0)
    if half:
        send_half(full)
    lax.fori_loop(0, 2, forward, 0)
    if row_heads:
        for side, copy in enumerate(row_halo(0)):
            copy.wait_recv()
            to_sibling(2 * side, 0).start()
    lax.fori_loop(2, wide, forward, 0)
    if reach_parts > 1:
        for copy in row_halo(1):
            copy.start()

    def row_pairs(part, frames):
        def heads(i, carry):
            for j in range(2):
                head = part * HALF + i * 2 + j
                o_row[head] = attend_row(q_row[head], kv_row, frames, head, table)
            return carry

        lax.fori_loop(0, HALF // 2, heads, 0)

    def row_part(part, frames):
        for f in frames:
            to_sibling(f, part).wait_recv()
        row_pairs(part, frames)

    if row_heads:
        own_row().wait()
        bytes_of(q_row, row_sem.at[1]).wait()
        row_part(0, (0, 1, 2))
    for part in range(2, row_parts):
        row_part(part, (1,))

    def attend_slot(s, kv_ref, first_frame):
        own_q(s).wait()

        def write(t, tile):
            o_stage[s, t] = tile

        position = s * TILES + spot

        def send(t):
            @pl.when(t == me)
            def _():
                pltpu.make_async_copy(o_stage.at[s, t], out.at[position], own_sem.at[2, s]).start()

            @pl.when(t != me)
            def _():
                remote(
                    o_stage.at[s, t], out.at[position], o_send.at[s], o_recv.at[s], seq, t
                ).start()

        attend(q_near.at[s], kv_ref, (scores_a, scores_b), write, send, table, s, first_frame)

    def wide_slot(s, carry):
        for copy in halo_copies(s):
            copy.wait_recv()
        attend_slot(s, kv_wide.at[s], 0)
        return carry

    def near_slot(s, carry):
        bytes_of(kv_near.at[s - wide, 0, pl.ds(0, TILES - 1)], kv_recv.at[s]).wait()
        own_kv(s, near_tile).wait()
        bytes_of(q_near.at[s, pl.ds(0, TILES - 1)], q_recv.at[s]).wait()
        attend_slot(s, kv_near.at[s - wide], 1)
        return carry

    near = slots - wide
    first = max(wide - near, 0)

    def pair(j, carry):
        if half:
            @pl.when((wide + j < full) | (column == 0))
            def _():
                near_slot(wide + j, 0)
        else:
            near_slot(wide + j, 0)
        wide_slot(first + j, 0)
        return carry

    bytes_of(q_near.at[wide_slots, pl.ds(0, TILES - 1)], q_recv.at[0]).wait()
    if first:
        lax.fori_loop(0, first, wide_slot, 0)
    if near:
        lax.fori_loop(0, near, pair, 0)

    if reach_parts > 1:
        for side, copy in enumerate(row_halo(1)):
            copy.wait_recv()
            to_sibling(2 * side, 1).start()
        row_part(1, (0, 1, 2))
    if row_heads:
        pltpu.make_async_copy(o_row, out.at[pl.ds(row_base, row_heads)], row_sem.at[2]).start()

    def own_out(s):
        return pltpu.make_async_copy(o_stage.at[s, me], out.at[s * TILES + spot], own_sem.at[2, s])

    def sent_inputs(s, count):
        bytes_of(kv_stage.at[pl.ds(s * TILES, count)], kv_send.at[s]).wait()

    def sent_queries(s, count):
        bytes_of(q_stage.at[s, pl.ds(0, count)], q_send.at[s]).wait()

    def got_outputs(s, count):
        bytes_of(out.at[pl.ds(s * TILES, count)], o_recv.at[s]).wait()

    def sent_outputs(s):
        own_out(s).wait()
        bytes_of(o_stage.at[s, pl.ds(0, TILES - 1)], o_send.at[s]).wait()

    def finish(s, carry):
        sent_inputs(s, TILES - 1)
        sent_outputs(s)
        got_outputs(s, TILES - 1)
        return carry

    def finish_queries(s, carry):
        sent_queries(s, TILES - 1)
        return carry

    def finish_halo(s, carry):
        for copy in halo_copies(s):
            copy.wait_send()
        return carry

    lax.fori_loop(0, wide, finish_halo, 0)
    for part in range(reach_parts):
        for copy in row_halo(part):
            copy.wait_send()
    for part in range(row_parts):
        for f in (0, 1, 2) if part < 2 else (1,):
            to_sibling(f, part).wait_send()
    if row_heads:
        pltpu.make_async_copy(o_row, out.at[pl.ds(row_base, row_heads)], row_sem.at[2]).wait()
    if half:
        @pl.when(column == 0)
        def _():
            sent_inputs(full, HALF - 1)
            sent_queries(full, HALF - 1)
            sent_outputs(full)
            got_outputs(full, HALF - 1)

        @pl.when(column == 1)
        def _():
            sent_inputs(full, HALF)
            sent_queries(full, HALF)
            got_outputs(full, HALF)
    bytes_of(q_stage.at[wide_slots, pl.ds(0, TILES - 1)], q_send.at[0]).wait()
    if full > wide:
        lax.fori_loop(wide, full, finish_queries, 0)
    lax.fori_loop(0, full, finish, 0)


def exchange(halves, wide, collective_id, frame_total, table, kv_stage, q_stage):
    slots = (halves + 1) // 2
    near = max(slots - wide, 1)
    row_heads = max(H - halves * HALF, 1)
    vmem = pl.BlockSpec(memory_space=pltpu.VMEM)
    bf16 = jnp.bfloat16
    tile = (TILE, HD)
    dma = pltpu.SemaphoreType.DMA
    scores = pltpu.VMEM((FRAMES * TILES * TILE, WT * TILE), jnp.float32)
    return pl.pallas_call(
        functools.partial(exchange_kernel, halves, wide, frame_total),
        out_shape=pltpu.VMEM((H,) + tile, bf16),
        in_specs=[pl.BlockSpec(memory_space=pltpu.SMEM), vmem, vmem],
        out_specs=vmem,
        scratch_shapes=[
            pltpu.VMEM((wide, FRAMES, TILES, 2) + tile, bf16),
            pltpu.VMEM((near, 1, TILES, 2) + tile, bf16),
            pltpu.VMEM((FRAMES, WT, row_heads, 2) + tile, bf16),
            pltpu.VMEM((slots, TILES) + tile, bf16),
            pltpu.VMEM((row_heads,) + tile, bf16),
            pltpu.VMEM((slots, TILES) + tile, bf16),
            pltpu.VMEM((row_heads,) + tile, bf16),
            scores, scores,
            dma((slots,)), dma((slots,)), dma((slots,)), dma((slots,)),
            dma((wide, 2)), dma((wide, 2)),
            dma((slots,)), dma((slots,)), dma((3, slots)),
            dma((2, 2)), dma((2, 2)),
            dma((FRAMES, ROW_HEADS // HALF)), dma((FRAMES, ROW_HEADS // HALF)),
            dma((3,)),
        ],
        compiler_params=pltpu.CompilerParams(
            collective_id=collective_id, has_side_effects=True, vmem_limit_bytes=40 << 20
        ),
        name=f"exchange_{halves}_{wide}",
    )(table, kv_stage, q_stage)


def power(exponent):
    return jnp.where(exponent > 0, 2.0, jnp.where(exponent < 0, 0.5, 1.0)).astype(jnp.float32)


def prepare_kernel(
    frame_total,
    extents_hbm, q_exp_hbm, k_exp_hbm, v_exp_hbm, q_data, k_data, v_data,
    table, place, plan, kv_stage, q_stage,
    extents, q_exp, k_exp, v_exp, order, q_in, k_in, v_in, in_sem, small_sem,
):
    loads = [
        pltpu.make_async_copy(src, dst, in_sem.at[i])
        for i, (src, dst) in enumerate(((k_data, k_in), (v_data, v_in), (q_data, q_in)))
    ]
    small = [
        pltpu.make_async_copy(src, dst, small_sem.at[i])
        for i, (src, dst) in enumerate(
            (
                (extents_hbm, extents),
                (k_exp_hbm, k_exp),
                (v_exp_hbm, v_exp),
                (q_exp_hbm, q_exp),
            )
        )
    ]
    for load in small + loads:
        load.start()
    for load in small:
        load.wait()

    zero = jnp.int32(0)
    one = jnp.int32(1)

    def flag(condition):
        return jnp.where(condition, one, zero)

    reach = [flag(extents[0, h] >= 1) for h in range(H)]
    flat = [flag(extents[1, h] <= 0) for h in range(H)]
    reaching = sum(reach, zero)
    flat_reaching = sum((r * f for r, f in zip(reach, flat)), zero)
    row_reaching = jnp.minimum(flat_reaching, ROW_REACH)
    row_most = row_reaching + sum(flat, zero) - flat_reaching
    row_count = zero
    for count in range(HALF, ROW_HEADS + 1, HALF):
        fits = reaching - jnp.minimum(row_reaching, count) <= PLANS[0][1] * TILES
        row_count = jnp.where(fits & (row_most >= count), count, row_count)
    row_reaching = jnp.minimum(row_reaching, row_count)
    row_base = H - row_count
    plan[0] = len(PLANS) - 1 - row_count // HALF
    next_reach, next_rest = zero, reaching - row_reaching
    next_row_reach, next_row_rest = zero, row_reaching
    for h in range(H):
        row_index = jnp.where(reach[h] > 0, next_row_reach, next_row_rest)
        row_end = jnp.where(reach[h] > 0, row_reaching, row_count)
        in_row = flat[h] * flag(row_index < row_end)
        outside = 1 - in_row
        other = jnp.where(reach[h] > 0, next_reach, next_rest)
        position = jnp.where(in_row > 0, row_base + row_index, other)
        next_row_reach += in_row * reach[h]
        next_row_rest += in_row * (1 - reach[h])
        next_reach += outside * reach[h]
        next_rest += outside * (1 - reach[h])
        order[position] = h
        place[h] = position
    me = lax.axis_index("head")
    seq = lax.axis_index("seq")
    column = lax.rem(me, WT)
    spot = column * HALF + me // WT

    def within(condition):
        return jnp.where(condition, 0.0, NEG).astype(jnp.float32)

    def beside(head, f):
        inside = (seq + f - 1 >= 0) & (seq + f - 1 < frame_total)
        return within((extents[0, head] >= abs(f - 1)) & inside)

    for s in range(SLOTS):
        head = order[s * TILES + spot]
        entry = s * ENTRIES
        for r in range(HT):
            for t in range(HT):
                table[entry + r * HT + t] = within(extents[1, head] >= abs(r - t))
        for c in range(WT):
            table[entry + HT * HT + c] = within(extents[2, head] >= c)
        for f in range(FRAMES):
            table[entry + HT * HT + WT + f] = beside(head, f)
    for i in range(ROW_HEADS):
        head = order[jnp.minimum(row_base + i, H - 1)]
        entry = ROW_TABLE + i * ROW_ENTRIES
        for c in range(WT):
            table[entry + c] = within(extents[2, head] >= jnp.abs(column - c))
        for f in range(FRAMES):
            table[entry + WT + f] = beside(head, f)


    def scaled(ref, exps, head):
        columns = pl.ds(pl.multiple_of(head * HD, HD), HD)
        return (ref[:, columns].astype(jnp.float32) * power(exps[0, head])).astype(jnp.bfloat16)

    def stage_keys(s, carry):
        for p in range(TILES):
            kv_stage[s * TILES + p, 0] = scaled(k_in, k_exp, order[s * TILES + p])
        return carry

    def stage_values(s, carry):
        for p in range(TILES):
            kv_stage[s * TILES + p, 1] = scaled(v_in, v_exp, order[s * TILES + p]).T
        return carry

    def stage_queries(s, carry):
        for p in range(TILES):
            q_stage[s, p] = scaled(q_in, q_exp, order[s * TILES + p])
        return carry

    for load, stage in zip(loads, (stage_keys, stage_values, stage_queries)):
        load.wait()
        lax.fori_loop(0, SLOTS, stage, 0)


def prepare(frame_total, extents, q_exp, k_exp, v_exp, q_data, k_data, v_data):
    smem = pl.BlockSpec(memory_space=pltpu.SMEM)
    bf16 = jnp.bfloat16
    kv = (H, 2, TILE, HD)
    q = (SLOTS, TILES, TILE, HD)
    vmem = pl.BlockSpec(memory_space=pltpu.VMEM)
    whole = pltpu.VMEM((TILE, H * HD), bf16)
    exponents = pltpu.SMEM((1, H), jnp.int32)
    return pl.pallas_call(
        functools.partial(prepare_kernel, frame_total),
        out_shape=(
            pltpu.SMEM((TABLE,), jnp.float32),
            pltpu.SMEM((H,), jnp.int32),
            pltpu.SMEM((1,), jnp.int32),
            pltpu.VMEM(kv, bf16),
            pltpu.VMEM(q, bf16),
        ),
        in_specs=[pl.BlockSpec(memory_space=pltpu.HBM)] * 7,
        out_specs=(smem, smem, smem, vmem, vmem),
        scratch_shapes=[
            pltpu.SMEM((3, H), jnp.int32),
            exponents, exponents, exponents,
            pltpu.SMEM((H,), jnp.int32),
            whole, whole, whole,
            pltpu.SemaphoreType.DMA((3,)),
            pltpu.SemaphoreType.DMA((4,)),
        ],
        compiler_params=pltpu.CompilerParams(vmem_limit_bytes=58 << 20),
        name="prepare",
    )(extents, q_exp, k_exp, v_exp, q_data, k_data, v_data)


def restore_kernel(place, tiles, out, sem):
    for h in range(H):
        pltpu.make_async_copy(tiles.at[place[h]], out.at[:, pl.ds(h * HD, HD)], sem).start()
    bytes_of(out, sem).wait()


def restore(place, tiles):
    return pl.pallas_call(
        restore_kernel,
        out_shape=pltpu.HBM((TILE, H * HD), jnp.bfloat16),
        in_specs=[
            pl.BlockSpec(memory_space=pltpu.SMEM),
            pl.BlockSpec(memory_space=pltpu.VMEM),
        ],
        out_specs=pl.BlockSpec(memory_space=pl.ANY),
        scratch_shapes=[pltpu.SemaphoreType.DMA(())],
        compiler_params=pltpu.CompilerParams(vmem_limit_bytes=40 << 20),
        name="restore",
    )(place, tiles)


def on_device(frame_total, q_data, k_data, v_data, q_exp, k_exp, v_exp, extents):
    table, place, plan, kv_stage, q_stage = prepare(
        frame_total, extents.T, q_exp, k_exp, v_exp, q_data, k_data, v_data
    )

    def branch(index, halves, wide):
        def run(table, place, kv_stage, q_stage):
            tiles = exchange(halves, wide, index, frame_total, table, kv_stage, q_stage)
            return restore(place, tiles)

        return run

    branches = [branch(i, *plan_sizes) for i, plan_sizes in enumerate(PLANS)]
    return lax.switch(plan[0], branches, table, place, kv_stage, q_stage)


def solution(mesh):
    rows = P(("seq", "head"), None)
    return jax.shard_map(
        functools.partial(on_device, mesh.shape["seq"]),
        mesh=mesh,
        in_specs=(rows,) * 6 + (P(),),
        out_specs=rows,
        check_vma=False,
    )
```
